512 devices in a mesh: xy: 128 (over y, z, core), gz: 4 (over x).
Axes of the slice: x: 4, y: 8, z: 8, core: 2. Of those that a mesh axis runs over, the one named last changes fastest.
Arguments:
- right_side: float32 [64, 128, 32, 128], P('gz', 'xy'), may hold values from -4.5 to 4.5
- phase: int32 [64, 128, 32, 128], P('gz', 'xy'), may hold values 0 or 1
- density_scale: float32 [64, 128, 32, 128], P('gz', 'xy'), may hold values from 0.5 to 2
Outputs:
- corrected: float32 [64, 128, 32, 128], P('gz', 'xy')
- coarse_correction: float32 [32, 128, 16, 64], P('gz', 'xy')
The draws below stay inside these ranges and needn't reach their ends.
All inputs are finite; a program needn't handle non-finite values. No bound on the sum of `phase` on one device may be relied on, other than what follows from the above.
Results may differ from the reference program's by a relative error of at most 0.00002.
Values sent between devices are 32-bit elements; how exact they have to be, the bound alone decides.
A program may use at most 128 MiB of HBM per device.

```python
import math
import jax
import jax.numpy as jnp

BX = 32
BY = 128
PY = 8
FINE_SWEEPS = 4
COARSE_SWEEPS = 8
NZ = 64
N_XY = 128


def draw_right_side(key, part):
    brick_shape = (NZ, N_XY, BX, BY)
    return jnp.clip(jax.random.normal(key, brick_shape, jnp.float32), -4.5, 4.5)


def plant(array, stream_key, least, top_value):
    index_at = [jax.random.randint(jax.random.fold_in(stream_key, axis), (), 0, length) for axis, length in enumerate(array.shape)]
    widest = array.shape.index(max(array.shape))
    beside = index_at[:widest] + [(index_at[widest] + 1) % array.shape[widest]] + index_at[widest + 1:]
    return array.at[tuple(index_at)].set(least).at[tuple(beside)].set(top_value)


def level_of(own_key, shape, pieces, smallest, high):
    def one(dim, parts):
        draws = jax.random.uniform(jax.random.fold_in(jax.random.fold_in(own_key, 6), dim), (parts,), jnp.float32, smallest / len(pieces), high / len(pieces))
        return jnp.repeat(jnp.exp(draws), shape[dim] // parts).reshape((-1,) + (1,) * (len(shape) - dim - 1))

    loudness = one(*pieces[0])
    for cut in pieces[1:]:
        loudness = loudness * one(*cut)
    return loudness


def setup_inputs(seed: int = 0) -> dict:
    key_of = jax.random.split(jax.random.key(seed), 4)
    return {
        "right_side": draw_right_side(jax.random.fold_in(key_of[3], 71), 0),
        "phase": plant((jax.random.randint(key_of[1], (NZ, N_XY, BX, BY), 0, 4) < 1).astype(jnp.int32), jax.random.fold_in(key_of[1], 1), 0, 1),
        "density_scale": jnp.clip(jnp.exp(math.log(2.0) - 1.3862944 * jax.random.uniform(key_of[2], (NZ, N_XY, BX, BY), jnp.float32) ** level_of(key_of[2], (NZ, N_XY, BX, BY), ((0, 4), (1, 128)), -0.2, 0.2)), 0.5, 2.0),
    }


def chebyshev_table(low_bound, sweeps):
    middle = 0.5 * (2.0 + low_bound)
    radius = 0.5 * (2.0 - low_bound)
    quotient = middle / radius
    previous = 1.0 / quotient
    coeffs = []
    for number in range(sweeps):
        current = 1.0 / (2.0 * quotient - previous)
        coeffs.append((current * previous, 2.0 * current / radius))
        previous = current
    return 1.0 / middle, coeffs


def to_grid(bricks):
    planes, count, lines, columns = bricks.shape
    rows = count // PY
    shaped = bricks.reshape(planes, rows, PY, lines, columns).transpose(0, 1, 3, 2, 4)
    return shaped.reshape(planes, rows * lines, PY * columns)


def to_bricks(grid, lines, columns):
    planes = grid.shape[0]
    rows = grid.shape[1] // lines
    shaped = grid.reshape(planes, rows, lines, PY, columns).transpose(0, 1, 3, 2, 4)
    return shaped.reshape(planes, rows * PY, lines, columns)


def pad_planes(field_in):
    return jnp.pad(field_in, ((1, 1), (1, 1), (0, 0)))


def face_weights(density_wide):
    center = density_wide[1:-1, 1:-1]
    padded_y = jnp.pad(center, ((0, 0), (0, 0), (1, 1)))
    neighbours = [density_wide[:-2, 1:-1], density_wide[2:, 1:-1], density_wide[1:-1, :-2],
                  density_wide[1:-1, 2:], padded_y[:, :, :-2], padded_y[:, :, 2:]]
    return jnp.stack([2.0 / (center + beside) for beside in neighbours])


def sum_faces(face_set):
    return face_set[0] + face_set[1] + face_set[2] + face_set[3] + face_set[4] + face_set[5]


def apply_operator(field_wide, face_set, diagonal):
    center = field_wide[1:-1, 1:-1]
    padded_y = jnp.pad(center, ((0, 0), (0, 0), (1, 1)))
    summed = face_set[0] * field_wide[:-2, 1:-1] + face_set[1] * field_wide[2:, 1:-1]
    summed = summed + face_set[2] * field_wide[1:-1, :-2] + face_set[3] * field_wide[1:-1, 2:]
    summed = summed + face_set[4] * padded_y[:, :, :-2] + face_set[5] * padded_y[:, :, 2:]
    return diagonal * center - summed


def chebyshev(source, face_set, diagonal, low_bound, sweeps):
    inverse_center, coeffs = chebyshev_table(low_bound, sweeps)
    iterate = jnp.zeros_like(source)
    residual = source
    search = (residual / diagonal) * inverse_center
    for number in range(sweeps):
        iterate = iterate + search
        residual = residual - apply_operator(pad_planes(search), face_set, diagonal)
        if number + 1 < sweeps:
            keep_part, push_part = coeffs[number]
            search = keep_part * search + push_part * (residual / diagonal)
    return iterate, residual


def restrict_cells(field_in):
    planes, lines, columns = field_in.shape
    blocks = field_in.reshape(planes // 2, 2, lines // 2, 2, columns // 2, 2)
    return jnp.sum(blocks, axis=(1, 3, 5)) * 0.125


def coarsen_faces(face_set):
    planes, lines, columns = face_set.shape[1:]
    half_planes, half_lines, half_columns = planes // 2, lines // 2, columns // 2
    low_z = face_set[0][0::2].reshape(half_planes, half_lines, 2, half_columns, 2).sum(axis=(2, 4))
    high_z = face_set[1][1::2].reshape(half_planes, half_lines, 2, half_columns, 2).sum(axis=(2, 4))
    low_x = face_set[2][:, 0::2].reshape(half_planes, 2, half_lines, half_columns, 2).sum(axis=(1, 4))
    high_x = face_set[3][:, 1::2].reshape(half_planes, 2, half_lines, half_columns, 2).sum(axis=(1, 4))
    low_y = face_set[4][:, :, 0::2].reshape(half_planes, 2, half_lines, 2, half_columns).sum(axis=(1, 3))
    high_y = face_set[5][:, :, 1::2].reshape(half_planes, 2, half_lines, 2, half_columns).sum(axis=(1, 3))
    return jnp.stack([low_z, high_z, low_x, high_x, low_y, high_y]) * 0.0625


def prolong_cells(coarse):
    planes, lines, columns = coarse.shape
    spread = jnp.broadcast_to(coarse[:, None, :, None, :, None], (planes, 2, lines, 2, columns, 2))
    return spread.reshape(planes * 2, lines * 2, columns * 2)


def reference(right_side, phase, density_scale):
    lines, columns = right_side.shape[2], right_side.shape[3]
    source = to_grid(right_side)
    density = to_grid(jnp.where(phase == 1, 1000.0, 1.0).astype(jnp.float32) * density_scale)
    face_set = face_weights(pad_planes(density))
    diagonal = sum_faces(face_set)
    smoothed, fine_residual = chebyshev(source, face_set, diagonal, 0.5, FINE_SWEEPS)
    coarse_rhs = restrict_cells(fine_residual)
    coarse_faces = coarsen_faces(face_set)
    coarse_diagonal = sum_faces(coarse_faces)
    coarse_field, coarse_residual = chebyshev(coarse_rhs, coarse_faces, coarse_diagonal, 0.1, COARSE_SWEEPS)
    corrected = smoothed + prolong_cells(coarse_field)
    return to_bricks(corrected, lines, columns), to_bricks(coarse_field, lines // 2, columns // 2)
```

```python
import jax
import jax.numpy as jnp
from jax import lax
from jax.experimental import pallas as pl
from jax.experimental.pallas import tpu as pltpu
from jax.sharding import PartitionSpec as P

PY = 8
FINE_SWEEPS = 4
COARSE_SWEEPS = 8

NZ, BX, BY = 16, 32, 128
HZ = 5
EZ, EX = NZ + 2 * HZ, BX + 16
X0 = 8
CZ, CX, CY = 8, 16, 64
KZ, KX = CZ + 16, CX + 16


def chebyshev_table(low_bound, sweeps):
    middle = 0.5 * (2.0 + low_bound)
    radius = 0.5 * (2.0 - low_bound)
    quotient = middle / radius
    previous = 1.0 / quotient
    coeffs = []
    for number in range(sweeps):
        current = 1.0 / (2.0 * quotient - previous)
        coeffs.append((current * previous, 2.0 * current / radius))
        previous = current
    return (1.0 / middle, coeffs)


def lanes_of(rows):
    return lax.broadcasted_iota(jnp.int32, (rows, 128), 1)


def guarded(total):
    return jnp.where(total > 0.0, 2.0 / total, 0.0)


def kernel(
    right_ref, phase_ref, scale_ref, out_ref, coarse_ref,
    e0, e1, s0, s1, fz0, fz1, fx0, fx1, fy0, fy1, ig0, ig1, xs,
    xsend, xrecv, pack, unpack, stage,
    cs, cr, csx, ys, yr, cx,
    send_sem, recv_sem,
):
    b = lax.axis_index("xy")
    g = lax.axis_index("gz")
    row, col = b // PY, b % PY
    n_rows = lax.axis_size("xy") // PY
    n_gz = lax.axis_size("gz")
    there = ((g > 0, g < n_gz - 1), (row > 0, row < n_rows - 1), (col > 0, col < PY - 1))

    def neighbour(axis, side):
        by = 1 if side else -1
        if axis == 0:
            return {"xy": b, "gz": g + by}
        return {"xy": b + by * (PY if axis == 1 else 1), "gz": g}

    def exchange(number, axis, sources, targets):
        copies = []
        for side in (0, 1):
            index = 2 * number + side
            copies.append(
                pltpu.make_async_remote_copy(
                    src_ref=sources[side], dst_ref=targets[side],
                    send_sem=send_sem.at[index], recv_sem=recv_sem.at[index],
                    device_id=neighbour(axis, side), device_id_type=pl.DeviceIdType.MESH,
                )
            )

        def start():
            for side in (0, 1):
                pl.when(there[axis][side])(copies[side].start)

        def wait():
            for side in (0, 1):
                pl.when(there[axis][1 - side])(copies[side].wait_recv)
            for side in (0, 1):
                pl.when(there[axis][side])(copies[side].wait_send)

        return start, wait

    @pl.loop(0, EZ)
    def _(p):
        for f in (0, 1):
            e0[f, p] = jnp.zeros((EX, 128), jnp.float32)

    barrier = pltpu.get_barrier_semaphore()
    count = jnp.int32(0)
    for axis in (0, 1, 2):
        for side in (0, 1):
            count = count + there[axis][side].astype(jnp.int32)

            @pl.when(there[axis][side])
            def _():
                pl.semaphore_signal(
                    barrier, inc=1, device_id=neighbour(axis, side),
                    device_id_type=pl.DeviceIdType.MESH,
                )

    @pl.loop(0, NZ)
    def _(z):
        heavy = jnp.where(phase_ref[z, 0] == 1, 1000.0, 1.0).astype(jnp.float32)
        e0[0, HZ + z, X0:X0 + BX] = heavy * scale_ref[z, 0]
        e0[1, HZ + z, X0:X0 + BX] = right_ref[z, 0]

    @pl.loop(0, KZ)
    def _(p):
        for f in range(4):
            cs[f, p] = jnp.zeros((KX, 128), jnp.float32)
        cr[p] = jnp.zeros((KX, 128), jnp.float32)

    for j in range(9):
        f, at = (0, j) if j < 5 else (1, j - 5)
        width = 5 - f
        xsend[0, j] = e0[f, HZ:HZ + NZ, X0 + at, :]
        xsend[1, j] = e0[f, HZ:HZ + NZ, X0 + BX - width + at, :]

    pl.semaphore_wait(barrier, count)

    start, wait = exchange(0, 1, (xsend.at[0], xsend.at[1]), (xrecv.at[0], xrecv.at[1]))
    start()
    wait()
    for side in (0, 1):
        @pl.when(there[1][1 - side])
        def _():
            for j in range(9):
                f, at = (0, j) if j < 5 else (1, j - 5)
                width = 5 - f
                to = X0 + BX + at if side == 0 else X0 - width + at
                e0[f, HZ:HZ + NZ, to, :] = xrecv[side, j]

    start, wait = exchange(
        1, 0,
        (e0.at[:, pl.ds(HZ, HZ)], e0.at[:, pl.ds(NZ, HZ)]),
        (e0.at[:, pl.ds(HZ + NZ, HZ)], e0.at[:, pl.ds(0, HZ)]),
    )
    start()
    wait()

    lane = lanes_of(EX)

    @pl.loop(0, EZ)
    def _(p):
        a, at = p // 8, (p % 8) * 16
        d, r = e0[0, p], e0[1, p]
        in_d = (lane >= at) & (lane < at + 8)
        in_r = (lane >= at + 8) & (lane < at + 16)
        for side, extra in ((0, 0), (1, 8)):
            rolled_d = pltpu.roll(d, (at + extra) % 128, 1)
            rolled_r = pltpu.roll(r, (at + extra + 8) % 128, 1)
            pack[side, a] = jnp.where(in_d, rolled_d, jnp.where(in_r, rolled_r, pack[side, a]))

    start, wait = exchange(2, 2, (pack.at[0], pack.at[1]), (unpack.at[0], unpack.at[1]))
    start()
    wait()

    @pl.loop(0, EZ)
    def _(p):
        a, at = p // 8, (p % 8) * 16
        right, left = unpack[0, a], unpack[1, a]
        use_right = (lane < 8) & there[2][1]
        use_left = (lane >= 120) & there[2][0]
        for f in (0, 1):
            low = pltpu.roll(right, (256 - at - 8 * f) % 128, 1)
            high = pltpu.roll(left, (256 - at - 8 * f - 8) % 128, 1)
            e1[f, p] = jnp.where(use_right, low, jnp.where(use_left, high, 0.0))

    def x_low(v):
        return pltpu.roll(v, 1, 0)

    def x_high(v):
        return pltpu.roll(v, v.shape[0] - 1, 0)

    def y_low(v0, v1):
        a0, a1 = pltpu.roll(v0, 1, 1), pltpu.roll(v1, 1, 1)
        return jnp.where(lane == 0, a1, a0), jnp.where(lane == 0, a0, a1)

    def y_high(v0, v1):
        a0, a1 = pltpu.roll(v0, 127, 1), pltpu.roll(v1, 127, 1)
        return jnp.where(lane == 127, a1, a0), jnp.where(lane == 127, a0, a1)

    center, coeffs = chebyshev_table(0.5, FINE_SWEEPS)
    fz0[1] = guarded(e0[0, 1] + e0[0, 0])
    fz1[1] = guarded(e1[0, 1] + e1[0, 0])

    @pl.loop(1, EZ - 1)
    def _(p):
        d0, d1 = e0[0, p], e1[0, p]
        up0, up1 = guarded(d0 + e0[0, p + 1]), guarded(d1 + e1[0, p + 1])
        fz0[p + 1], fz1[p + 1] = up0, up1
        w0, w1 = guarded(d0 + x_low(d0)), guarded(d1 + x_low(d1))
        fx0[p], fx1[p] = w0, w1
        l0, l1 = y_low(d0, d1)
        v0, v1 = guarded(d0 + l0), guarded(d1 + l1)
        fy0[p], fy1[p] = v0, v1
        h0, h1 = y_high(v0, v1)
        g0 = fz0[p] + up0 + w0 + x_high(w0) + v0 + h0
        g1 = fz1[p] + up1 + w1 + x_high(w1) + v1 + h1
        i0 = jnp.where(d0 > 0.0, 1.0 / g0, 0.0)
        i1 = jnp.where(d1 > 0.0, 1.0 / g1, 0.0)
        ig0[p], ig1[p] = i0, i1
        s0[p] = e0[1, p] * i0 * center
        s1[p] = e1[1, p] * i1 * center

    dot_kw = dict(preferred_element_type=jnp.float32, precision=lax.Precision.HIGHEST)
    from_lane = lax.broadcasted_iota(jnp.int32, (128, 128), 0)
    to_lane = lax.broadcasted_iota(jnp.int32, (128, 128), 1)
    pairs = jnp.where(from_lane // 2 == to_lane, 1.0, 0.0).astype(jnp.float32)
    evens = jnp.where(from_lane == 2 * to_lane, 1.0, 0.0).astype(jnp.float32)
    both = evens + jnp.where((from_lane == 2 * to_lane + 2) & (to_lane < CY), 1.0, 0.0).astype(jnp.float32)

    def row_pairs(ref, p):
        return ref[p, pl.ds(X0, CX, stride=2), :] + ref[p, pl.ds(X0 + 1, CX, stride=2), :]

    @pl.loop(0, CZ)
    def _(c):
        p = HZ + 2 * c
        rows = pl.ds(pl.multiple_of(c * CX, CX), CX)
        low_z, high_z = row_pairs(fz0, p), row_pairs(fz0, p + 2)
        low_x = fx0[p, pl.ds(X0, CX, stride=2), :] + fx0[p + 1, pl.ds(X0, CX, stride=2), :]
        high_x = fx0[p, pl.ds(X0 + 2, CX, stride=2), :] + fx0[p + 1, pl.ds(X0 + 2, CX, stride=2), :]
        stage[0, rows] = low_z
        stage[1, rows] = low_x
        stage[2, rows] = low_z + high_z + low_x + high_x
        stage[3, rows] = row_pairs(fy0, p) + row_pairs(fy0, p + 1)
        stage[4, rows] = row_pairs(fy1, p) + row_pairs(fy1, p + 1)

    wide = lanes_of(CZ * CX)
    last = jnp.where(wide == CY - 1, pltpu.roll(stage[4], CY - 1, 1), 0.0)
    total = jnp.dot(stage[2], pairs, **dot_kw) + jnp.dot(stage[3], both, **dot_kw) + last
    whole = (
        total,
        jnp.dot(stage[0], pairs, **dot_kw),
        jnp.dot(stage[1], pairs, **dot_kw),
        jnp.dot(stage[3], evens, **dot_kw),
    )
    for f in range(4):
        ys[f] = (whole[f] * 0.0625).reshape(CZ, CX, 128)

    start_y, wait_y = exchange(3, 2, (ys.at[pl.ds(0, 4)],) * 2, (yr.at[0, pl.ds(0, 4)], yr.at[1, pl.ds(0, 4)]))
    start_y()

    def sweep(k):
        first, last_plane = 2 + k, EZ - 2 - k
        keep, push = coeffs[k]

        def step(p, carry):
            c0, c1, f0, f1 = carry
            n0, n1 = s0[p + 1], s1[p + 1]
            g0 = fz0[p + 1] * (n0 - c0)
            g1 = fz1[p + 1] * (n1 - c1)
            a0 = fx0[p] * (c0 - x_low(c0))
            a1 = fx1[p] * (c1 - x_low(c1))
            l0, l1 = y_low(c0, c1)
            b0 = fy0[p] * (c0 - l0)
            b1 = fy1[p] * (c1 - l1)
            h0, h1 = y_high(b0, b1)
            r0 = e0[1, p] - ((f0 - g0) + (a0 - x_high(a0)) + (b0 - h0))
            r1 = e1[1, p] - ((f1 - g1) + (a1 - x_high(a1)) + (b1 - h1))
            e0[1, p] = r0
            mine = c0[X0:X0 + BX]
            xs[p] = mine if k == 0 else xs[p] + mine
            if k + 1 < FINE_SWEEPS:
                e1[1, p] = r1
                s0[p] = keep * c0 + push * (r0 * ig0[p])
                s1[p] = keep * c1 + push * (r1 * ig1[p])
            return n0, n1, g0, g1

        c0, c1 = s0[first], s1[first]
        lax.fori_loop(
            first, last_plane, step,
            (c0, c1, fz0[first] * (c0 - s0[first - 1]), fz1[first] * (c1 - s1[first - 1])),
        )

    clane = lanes_of(CX)

    def merge(f, target):
        @pl.loop(0, CZ)
        def _(z):
            right = jnp.where(there[2][1], pltpu.roll(yr[0, f, z], 64, 1), 0.0)
            left = jnp.where(there[2][0], pltpu.roll(yr[1, f, z], 64, 1), 0.0)
            target[8 + z, 8:8 + CX] = jnp.where(
                clane < CY, ys[f, z], jnp.where(clane < 96, right, left)
            )

    sweep(0)
    sweep(1)
    wait_y()
    for f in range(4):
        merge(f, cs.at[f])
    start_x, wait_x = exchange(
        4, 1,
        (cs.at[:, pl.ds(8, CZ), pl.ds(8, 8)], cs.at[:, pl.ds(8, CZ), pl.ds(16, 8)]),
        (cs.at[:, pl.ds(8, CZ), pl.ds(24, 8)], cs.at[:, pl.ds(8, CZ), pl.ds(0, 8)]),
    )
    start_x()
    sweep(2)
    sweep(3)

    @pl.loop(0, CZ)
    def _(c):
        p = HZ + 2 * c
        rows = pl.ds(pl.multiple_of(c * CX, CX), CX)
        stage[0, rows] = row_pairs(e0.at[1], p) + row_pairs(e0.at[1], p + 1)

    ys[4] = (jnp.dot(stage[0], pairs, **dot_kw) * 0.125).reshape(CZ, CX, 128)
    start_y, wait_y = exchange(5, 2, (ys.at[4],) * 2, (yr.at[0, 4], yr.at[1, 4]))
    start_y()
    wait_x()
    start_z, wait_z = exchange(
        6, 0,
        (cs.at[:, pl.ds(8, 8)], cs.at[:, pl.ds(8, 8)]),
        (cs.at[:, pl.ds(16, 8)], cs.at[:, pl.ds(0, 8)]),
    )
    start_z()
    wait_y()
    merge(4, cr)
    start_x, wait_x = exchange(
        7, 1,
        (cr.at[pl.ds(8, CZ), pl.ds(8, 8)], cr.at[pl.ds(8, CZ), pl.ds(16, 8)]),
        (cr.at[pl.ds(8, CZ), pl.ds(24, 8)], cr.at[pl.ds(8, CZ), pl.ds(0, 8)]),
    )
    start_x()
    wait_x()
    start_r, wait_r = exchange(
        8, 0, (cr.at[pl.ds(8, 8)], cr.at[pl.ds(8, 8)]), (cr.at[pl.ds(16, 8)], cr.at[pl.ds(0, 8)])
    )
    start_r()
    wait_z()
    wait_r()

    center, ccoeffs = chebyshev_table(0.1, COARSE_SWEEPS)

    @pl.loop(1, KZ - 1)
    def _(p):
        diagonal = cs[0, p]
        inverse = jnp.where(diagonal > 0.0, 1.0 / diagonal, 0.0)
        csx[0, p] = inverse
        csx[1, p] = cr[p] * inverse * center

    def coarse_sweep(k):
        first, last_plane = 2 + k, KZ - 2 - k
        keep, push = ccoeffs[k]

        def step(p, carry):
            below, here = carry
            above = csx[1, p + 1]
            fx, fy = cs[2, p], cs[3, p]
            summed = cs[1, p] * below + cs[1, p + 1] * above
            summed = summed + fx * x_low(here) + x_high(fx * here)
            summed = summed + fy * pltpu.roll(here, 1, 1) + pltpu.roll(fy * here, 127, 1)
            r = cr[p] - (cs[0, p] * here - summed)
            cr[p] = r
            csx[1, p] = keep * here + push * (r * csx[0, p])
            return here, above

        lax.fori_loop(first, last_plane, step, (csx[1, first - 1], csx[1, first]))

    for k in range(COARSE_SWEEPS):
        @pl.loop(0, CZ)
        def _(z):
            mine = csx[1, 8 + z, 8:8 + CX]
            cx[z] = mine if k == 0 else cx[z] + mine
        if k + 1 < COARSE_SWEEPS:
            coarse_sweep(k)

    spread = jnp.where(to_lane // 2 == from_lane, 1.0, 0.0).astype(jnp.float32)
    stage[1] = jnp.dot(cx[...].reshape(CZ * CX, 128), spread, **dot_kw)

    @pl.loop(0, CZ)
    def _(c):
        coarse_ref[c, 0] = cx[c, :, 0:CY]
        wide_rows = stage[1, pl.ds(pl.multiple_of(c * CX, CX), CX), :]
        stage[2, pl.ds(0, CX, stride=2), :] = wide_rows
        stage[2, pl.ds(1, CX, stride=2), :] = wide_rows
        twice = stage[2, 0:BX, :]
        for i in (0, 1):
            out_ref[2 * c + i, 0] = xs[HZ + 2 * c + i] + twice


def body(right_side, phase, density_scale):
    fine = pltpu.VMEM((EZ, EX, 128), jnp.float32)
    return pl.pallas_call(
        kernel,
        out_shape=(
            jax.ShapeDtypeStruct((NZ, 1, BX, BY), jnp.float32),
            jax.ShapeDtypeStruct((CZ, 1, CX, CY), jnp.float32),
        ),
        in_specs=[pl.BlockSpec(memory_space=pltpu.VMEM)] * 3,
        out_specs=(pl.BlockSpec(memory_space=pltpu.VMEM),) * 2,
        scratch_shapes=[
            pltpu.VMEM((2, EZ, EX, 128), jnp.float32),
            pltpu.VMEM((2, EZ, EX, 128), jnp.float32),
            *([fine] * 10),
            pltpu.VMEM((EZ, BX, 128), jnp.float32),
            pltpu.VMEM((2, 9, NZ, 128), jnp.float32),
            pltpu.VMEM((2, 9, NZ, 128), jnp.float32),
            pltpu.VMEM((2, 4, EX, 128), jnp.float32),
            pltpu.VMEM((2, 4, EX, 128), jnp.float32),
            pltpu.VMEM((5, CZ * CX, 128), jnp.float32),
            pltpu.VMEM((4, KZ, KX, 128), jnp.float32),
            pltpu.VMEM((KZ, KX, 128), jnp.float32),
            pltpu.VMEM((2, KZ, KX, 128), jnp.float32),
            pltpu.VMEM((5, CZ, CX, 128), jnp.float32),
            pltpu.VMEM((2, 5, CZ, CX, 128), jnp.float32),
            pltpu.VMEM((CZ, CX, 128), jnp.float32),
            pltpu.SemaphoreType.DMA((18,)),
            pltpu.SemaphoreType.DMA((18,)),
        ],
        compiler_params=pltpu.CompilerParams(
            collective_id=0, has_side_effects=True, vmem_limit_bytes=40 << 20
        ),
        name="vcycle",
    )(right_side, phase, density_scale)


def solution(mesh):
    placed = P("gz", "xy", None, None)
    return jax.shard_map(
        body,
        mesh=mesh,
        in_specs=(placed, placed, placed),
        out_specs=(placed, placed),
        check_vma=False,
    )
```

```python
import jax
import jax.numpy as jnp
from jax import lax
from jax.experimental import pallas as pl
from jax.experimental.pallas import tpu as pltpu
from jax.sharding import PartitionSpec as P

PY = 8
FINE_SWEEPS = 4
COARSE_SWEEPS = 8

NZ, BX, BY = 16, 32, 128
HZ = 5
EZ, EX = NZ + 2 * HZ, BX + 16
X0 = 8
CZ, CX, CY = 8, 16, 64
KZ, KX = CZ + 16, CX + 16


def chebyshev_table(low_bound, sweeps):
    middle = 0.5 * (2.0 + low_bound)
    radius = 0.5 * (2.0 - low_bound)
    quotient = middle / radius
    previous = 1.0 / quotient
    coeffs = []
    for number in range(sweeps):
        current = 1.0 / (2.0 * quotient - previous)
        coeffs.append((current * previous, 2.0 * current / radius))
        previous = current
    return (1.0 / middle, coeffs)


def lanes_of(rows):
    return lax.broadcasted_iota(jnp.int32, (rows, 128), 1)


def face(total):
    return 2.0 / jnp.maximum(total, 1e-3)


def kernel(
    right_ref, phase_ref, scale_ref, out_ref, coarse_ref,
    e0, e1, s0, s1, r0, r1, fz0, fz1, fx0, fx1, fy0, fy1, gy0, gy1, ig0, ig1,
    xsend, xrecv, pack, unpack, stage,
    cs, cr, ci, sx, rx, ys, yr, cx,
    send_sem, recv_sem,
):
    b = lax.axis_index("xy")
    g = lax.axis_index("gz")
    row, col = b // PY, b % PY
    n_rows = lax.axis_size("xy") // PY
    n_gz = lax.axis_size("gz")
    there = ((g > 0, g < n_gz - 1), (row > 0, row < n_rows - 1), (col > 0, col < PY - 1))

    def neighbour(axis, side):
        by = 1 if side else -1
        if axis == 0:
            return {"xy": b, "gz": g + by}
        return {"xy": b + by * (PY if axis == 1 else 1), "gz": g}

    def exchange(number, axis, sources, targets):
        copies = []
        for side in (0, 1):
            index = 2 * number + side
            copies.append(
                pltpu.make_async_remote_copy(
                    src_ref=sources[side], dst_ref=targets[side],
                    send_sem=send_sem.at[index], recv_sem=recv_sem.at[index],
                    device_id=neighbour(axis, side), device_id_type=pl.DeviceIdType.MESH,
                )
            )

        def start():
            for side in (0, 1):
                pl.when(there[axis][side])(copies[side].start)

        def wait():
            for side in (0, 1):
                pl.when(there[axis][1 - side])(copies[side].wait_recv)
            for side in (0, 1):
                pl.when(there[axis][side])(copies[side].wait_send)

        return start, wait

    for f in (0, 1):
        for p in range(EZ):
            if HZ <= p < HZ + NZ:
                e0[f, p, 0:X0] = jnp.zeros((X0, 128), jnp.float32)
                e0[f, p, X0 + BX:EX] = jnp.zeros((EX - X0 - BX, 128), jnp.float32)
            else:
                e0[f, p] = jnp.zeros((EX, 128), jnp.float32)

    barrier = pltpu.get_barrier_semaphore()
    count = jnp.int32(0)
    for axis in (0, 1, 2):
        for side in (0, 1):
            count = count + there[axis][side].astype(jnp.int32)

            @pl.when(there[axis][side])
            def _():
                pl.semaphore_signal(
                    barrier, inc=1, device_id=neighbour(axis, side),
                    device_id_type=pl.DeviceIdType.MESH,
                )

    for z in range(NZ):
        heavy = jnp.where(phase_ref[z, 0] == 1, 1000.0, 1.0).astype(jnp.float32)
        e0[0, HZ + z, X0:X0 + BX] = heavy * scale_ref[z, 0]
        e0[1, HZ + z, X0:X0 + BX] = right_ref[z, 0]

    @pl.loop(0, KZ)
    def _(p):
        for f in range(4):
            cs[f, p] = jnp.zeros((KX + 8, 128), jnp.float32)
        cr[p] = jnp.zeros((KX + 8, 128), jnp.float32)

    for j in range(9):
        f, at = (0, j) if j < 5 else (1, j - 5)
        width = 5 - f
        xsend[0, j] = e0[f, HZ:HZ + NZ, X0 + at, :]
        xsend[1, j] = e0[f, HZ:HZ + NZ, X0 + BX - width + at, :]

    pl.semaphore_wait(barrier, count)

    start, wait = exchange(0, 1, (xsend.at[0], xsend.at[1]), (xrecv.at[0], xrecv.at[1]))
    start()
    wait()
    for side in (0, 1):
        @pl.when(there[1][1 - side])
        def _():
            for j in range(9):
                f, at = (0, j) if j < 5 else (1, j - 5)
                width = 5 - f
                to = X0 + BX + at if side == 0 else X0 - width + at
                e0[f, HZ:HZ + NZ, to, :] = xrecv[side, j]

    start, wait = exchange(
        1, 0,
        (e0.at[:, pl.ds(HZ, HZ)], e0.at[:, pl.ds(NZ, HZ)]),
        (e0.at[:, pl.ds(HZ + NZ, HZ)], e0.at[:, pl.ds(0, HZ)]),
    )
    start()
    wait()

    lane = lanes_of(EX)

    for a in range(4):
        packed = [None, None]
        for i in range(min(8, EZ - 8 * a)):
            for f in (0, 1):
                v = e0[f, 8 * a + i]
                at = 16 * i + 8 * f
                for side in (0, 1):
                    rolled = pltpu.roll(v, (at + 8 * side) % 128, 1)
                    packed[side] = rolled if packed[side] is None else jnp.where(lane < at, packed[side], rolled)
        pack[0, a], pack[1, a] = packed

    start, wait = exchange(2, 2, (pack.at[0], pack.at[1]), (unpack.at[0], unpack.at[1]))
    start()
    wait()

    use_right = (lane < 8) & there[2][1]
    use_left = (lane >= 120) & there[2][0]
    for a in range(4):
        right, left = unpack[0, a], unpack[1, a]
        for i in range(min(8, EZ - 8 * a)):
            for f in (0, 1):
                at = 16 * i + 8 * f
                low = pltpu.roll(right, (128 - at) % 128, 1)
                high = pltpu.roll(left, (120 - at) % 128, 1)
                e1[f, 8 * a + i] = jnp.where(use_right, low, jnp.where(use_left, high, 0.0))

    lane8 = lanes_of(8)

    def y_low(v):
        a0, a1 = pltpu.roll(v[0], 1, 1), pltpu.roll(v[1], 1, 1)
        return jnp.where(lane8 == 0, a1, a0), jnp.where(lane8 == 0, a0, a1)

    def y_high(v):
        a0, a1 = pltpu.roll(v[0], 127, 1), pltpu.roll(v[1], 127, 1)
        return jnp.where(lane8 == 127, a1, a0), jnp.where(lane8 == 127, a0, a1)

    center, coeffs = chebyshev_table(0.5, FINE_SWEEPS)
    es, fzs, fxs, fys, gys, igs = (e0, e1), (fz0, fz1), (fx0, fx1), (fy0, fy1), (gy0, gy1), (ig0, ig1)

    def at_rows(refs, p, r, *lead):
        return [ref[(*lead, p, pl.ds(r, 8))] for ref in refs]

    tiles = [4 + 8 * i for i in range(5)]

    def faces_step(p, below):
        out = []
        for i, r in enumerate(tiles):
            d = at_rows(es, p, r, 0)
            above = at_rows(es, p + 1, r, 0)
            before = at_rows(es, p, r - 1, 0)
            after = at_rows(es, p, r + 1, 0)
            left, right = y_low(d), y_high(d)
            for t in (0, 1):
                up = face(d[t] + above[t])
                w, e = face(d[t] + before[t]), face(d[t] + after[t])
                v, h = face(d[t] + left[t]), face(d[t] + right[t])
                inverse = jnp.where(d[t] > 0.0, 1.0 / (below[2 * i + t] + up + w + e + v + h), 0.0)
                fzs[t][p + 1, pl.ds(r, 8)] = up
                fxs[t][p, pl.ds(r, 8)] = w
                if r == tiles[-1]:
                    fxs[t][p, pl.ds(r + 1, 8)] = e
                fys[t][p, pl.ds(r, 8)] = v
                gys[t][p, pl.ds(r, 8)] = h
                igs[t][p, pl.ds(r, 8)] = inverse
                ss[t][0, p, pl.ds(r, 8)] = es[t][1, p, pl.ds(r, 8)] * inverse * center
                out.append(up)
        return tuple(out)

    ss, rs = (s0, s1), (r0, r1)
    below = []
    for r in tiles:
        d, above = at_rows(es, 0, r, 0), at_rows(es, 1, r, 0)
        for t in (0, 1):
            up = face(d[t] + above[t])
            fzs[t][1, pl.ds(r, 8)] = up
            below.append(up)
    lax.fori_loop(1, EZ - 1, faces_step, tuple(below))

    dot_kw = dict(preferred_element_type=jnp.float32, precision=lax.Precision.HIGHEST)
    from_lane = lax.broadcasted_iota(jnp.int32, (128, 128), 0)
    to_lane = lax.broadcasted_iota(jnp.int32, (128, 128), 1)
    pairs = jnp.where(from_lane // 2 == to_lane, 1.0, 0.0).astype(jnp.float32)
    evens = jnp.where(from_lane == 2 * to_lane, 1.0, 0.0).astype(jnp.float32)
    both = evens + jnp.where((from_lane == 2 * to_lane + 2) & (to_lane < CY), 1.0, 0.0).astype(jnp.float32)

    def row_pairs(ref, p):
        return ref[p, pl.ds(X0, CX, stride=2), :] + ref[p, pl.ds(X0 + 1, CX, stride=2), :]

    for c in range(CZ):
        p = HZ + 2 * c
        rows = pl.ds(c * CX, CX)
        low_z, high_z = row_pairs(fz0, p), row_pairs(fz0, p + 2)
        low_x = fx0[p, pl.ds(X0, CX, stride=2), :] + fx0[p + 1, pl.ds(X0, CX, stride=2), :]
        high_x = fx0[p, pl.ds(X0 + 2, CX, stride=2), :] + fx0[p + 1, pl.ds(X0 + 2, CX, stride=2), :]
        stage[0, rows] = low_z
        stage[1, rows] = low_x
        stage[2, rows] = low_z + high_z + low_x + high_x
        stage[3, rows] = row_pairs(fy0, p) + row_pairs(fy0, p + 1)
        stage[4, rows] = row_pairs(fy1, p) + row_pairs(fy1, p + 1)

    wide = lanes_of(CZ * CX)
    last = jnp.where(wide == CY - 1, pltpu.roll(stage[4], CY - 1, 1), 0.0)
    total = jnp.dot(stage[2], pairs, **dot_kw) + jnp.dot(stage[3], both, **dot_kw) + last
    whole = (
        total,
        jnp.dot(stage[0], pairs, **dot_kw),
        jnp.dot(stage[1], pairs, **dot_kw),
        jnp.dot(stage[3], evens, **dot_kw),
    )
    for f in range(4):
        ys[f] = (whole[f] * 0.0625).reshape(CZ, CX, 128)

    start_y, wait_y = exchange(3, 2, (ys.at[pl.ds(0, 4)],) * 2, (yr.at[0, pl.ds(0, 4)], yr.at[1, pl.ds(0, 4)]))
    start_y()

    def sweep(k):
        first, end = 2 + k, EZ - 2 - k
        keep, push = coeffs[k]
        rows_of = tiles if k + 1 < FINE_SWEEPS else [X0 + 8 * i for i in range(4)]
        lanes = (0, 1) if k + 1 < FINE_SWEEPS else (0,)
        source = (lambda t, p, r: es[t][1, p, pl.ds(r, 8)]) if k == 0 else (lambda t, p, r: rs[t][k - 1, p, pl.ds(r, 8)])

        def step(j, fluxes):
            fluxes = list(fluxes)
            for i, r in enumerate(rows_of):
                for u in (0, 1):
                    p = first + 2 * j + u
                    c = at_rows(ss, p, r, k)
                    left, right = y_low(c), y_high(c)
                    for t in lanes:
                        up = fzs[t][p + 1, pl.ds(r, 8)] * (ss[t][k, p + 1, pl.ds(r, 8)] - c[t])
                        total = fluxes[len(lanes) * i + t] - up
                        total = total + fxs[t][p, pl.ds(r, 8)] * (c[t] - ss[t][k, p, pl.ds(r - 1, 8)])
                        total = total + fxs[t][p, pl.ds(r + 1, 8)] * (c[t] - ss[t][k, p, pl.ds(r + 1, 8)])
                        total = total + fys[t][p, pl.ds(r, 8)] * (c[t] - left[t])
                        total = total + gys[t][p, pl.ds(r, 8)] * (c[t] - right[t])
                        residual = source(t, p, r) - total
                        rs[t][k, p, pl.ds(r, 8)] = residual
                        if k + 1 < FINE_SWEEPS:
                            ss[t][k + 1, p, pl.ds(r, 8)] = keep * c[t] + (push * residual) * igs[t][p, pl.ds(r, 8)]
                        fluxes[len(lanes) * i + t] = up
            return tuple(fluxes)

        fluxes = []
        for r in rows_of:
            for t in lanes:
                fluxes.append(
                    fzs[t][first, pl.ds(r, 8)] * (ss[t][k, first, pl.ds(r, 8)] - ss[t][k, first - 1, pl.ds(r, 8)])
                )
        lax.fori_loop(0, (end - first) // 2, step, tuple(fluxes))

    clane = lanes_of(CX)

    def merge(f, target):
        for z in range(CZ):
            right = jnp.where(there[2][1], pltpu.roll(yr[0, f, z], 64, 1), 0.0)
            left = jnp.where(there[2][0], pltpu.roll(yr[1, f, z], 64, 1), 0.0)
            target[8 + z, 8:8 + CX] = jnp.where(
                clane < CY, ys[f, z], jnp.where(clane < 96, right, left)
            )

    sweep(0)
    sweep(1)
    wait_y()
    for f in range(4):
        merge(f, cs.at[f])
    start_x, wait_x = exchange(
        4, 1,
        (cs.at[:, pl.ds(8, CZ), pl.ds(8, 8)], cs.at[:, pl.ds(8, CZ), pl.ds(16, 8)]),
        (cs.at[:, pl.ds(8, CZ), pl.ds(24, 8)], cs.at[:, pl.ds(8, CZ), pl.ds(0, 8)]),
    )
    start_x()
    sweep(2)
    sweep(3)

    last_residual = rs[0].at[FINE_SWEEPS - 1]
    for c in range(CZ):
        p = HZ + 2 * c
        stage[0, pl.ds(c * CX, CX)] = row_pairs(last_residual, p) + row_pairs(last_residual, p + 1)

    ys[4] = (jnp.dot(stage[0], pairs, **dot_kw) * 0.125).reshape(CZ, CX, 128)
    start_y, wait_y = exchange(5, 2, (ys.at[4],) * 2, (yr.at[0, 4], yr.at[1, 4]))
    start_y()
    wait_x()
    start_z, wait_z = exchange(
        6, 0,
        (cs.at[:, pl.ds(8, 8), pl.ds(0, KX)], cs.at[:, pl.ds(8, 8), pl.ds(0, KX)]),
        (cs.at[:, pl.ds(16, 8), pl.ds(0, KX)], cs.at[:, pl.ds(0, 8), pl.ds(0, KX)]),
    )
    start_z()
    wait_y()
    merge(4, cr)
    start_x, wait_x = exchange(
        7, 1,
        (cr.at[pl.ds(8, CZ), pl.ds(8, 8)], cr.at[pl.ds(8, CZ), pl.ds(16, 8)]),
        (cr.at[pl.ds(8, CZ), pl.ds(24, 8)], cr.at[pl.ds(8, CZ), pl.ds(0, 8)]),
    )
    start_x()
    wait_x()
    start_r, wait_r = exchange(
        8, 0, (cr.at[pl.ds(8, 8), pl.ds(0, KX)], cr.at[pl.ds(8, 8), pl.ds(0, KX)]), (cr.at[pl.ds(16, 8), pl.ds(0, KX)], cr.at[pl.ds(0, 8), pl.ds(0, KX)])
    )
    start_r()
    wait_z()
    wait_r()

    center, ccoeffs = chebyshev_table(0.1, COARSE_SWEEPS)

    for p in range(1, KZ - 1):
        diagonal = cs[0, p, 0:KX]
        inverse = jnp.where(diagonal > 0.0, 1.0 / diagonal, 0.0)
        ci[p, 0:KX] = inverse
        sx[0, p, 0:KX] = cr[p, 0:KX] * inverse * center

    def coarse_sweep(k):
        halo = COARSE_SWEEPS - 2 - k
        first, count = 8 - halo, CZ + 2 * halo
        n_tiles = (CX + 2 * halo + 7) // 8
        r_first = min(8 - halo, KX + 7 - 8 * n_tiles)
        rows_of = [r_first + 8 * i for i in range(n_tiles)]
        keep, push = ccoeffs[k]
        unroll = 4 if count % 4 == 0 else 2

        def step(j, fluxes):
            fluxes = list(fluxes)
            for i, r in enumerate(rows_of):
                rows = pl.ds(r, 8)
                for u in range(unroll):
                    p = first + unroll * j + u
                    c = sx[k, p, rows]
                    above = sx[k, p + 1, rows]
                    fz = cs[1, p + 1, rows]
                    fy = cs[3, p, rows]
                    total = cs[0, p, rows] * c - fluxes[i] - fz * above
                    total = total - cs[2, p, rows] * sx[k, p, pl.ds(r - 1, 8)]
                    total = total - cs[2, p, pl.ds(r + 1, 8)] * sx[k, p, pl.ds(r + 1, 8)]
                    total = total - fy * pltpu.roll(c, 1, 1) - pltpu.roll(fy * c, 127, 1)
                    residual = (cr if k == 0 else rx.at[k])[p, rows] - total
                    if k + 2 < COARSE_SWEEPS:
                        rx[k + 1, p, rows] = residual
                    sx[k + 1, p, rows] = keep * c + (push * residual) * ci[p, rows]
                    fluxes[i] = fz * c
            return tuple(fluxes)

        lax.fori_loop(
            0, count // unroll, step,
            tuple(cs[1, first, pl.ds(r, 8)] * sx[k, first - 1, pl.ds(r, 8)] for r in rows_of),
        )

    for k in range(COARSE_SWEEPS - 1):
        coarse_sweep(k)
    for z in range(CZ):
        mine = sx[0, 8 + z, 8:8 + CX]
        for k in range(1, COARSE_SWEEPS):
            mine = mine + sx[k, 8 + z, 8:8 + CX]
        cx[z] = mine

    spread = jnp.where(to_lane // 2 == from_lane, 1.0, 0.0).astype(jnp.float32)
    stage[1] = jnp.dot(cx[...].reshape(CZ * CX, 128), spread, **dot_kw)

    for c in range(CZ):
        coarse_ref[c, 0] = cx[c, :, 0:CY]
        wide_rows = stage[1, pl.ds(c * CX, CX), :]
        spot = pl.ds(BX * (c % 2), CX, stride=2), pl.ds(BX * (c % 2) + 1, CX, stride=2)
        stage[2, spot[0], :] = wide_rows
        stage[2, spot[1], :] = wide_rows
        twice = stage[2, pl.ds(BX * (c % 2), BX), :]
        for i in (0, 1):
            mine = s0[0, HZ + 2 * c + i, X0:X0 + BX]
            for k in range(1, FINE_SWEEPS):
                mine = mine + s0[k, HZ + 2 * c + i, X0:X0 + BX]
            out_ref[2 * c + i, 0] = mine + twice


def body(right_side, phase, density_scale):
    fine = pltpu.VMEM((EZ, EX, 128), jnp.float32)
    return pl.pallas_call(
        kernel,
        out_shape=(
            jax.ShapeDtypeStruct((NZ, 1, BX, BY), jnp.float32),
            jax.ShapeDtypeStruct((CZ, 1, CX, CY), jnp.float32),
        ),
        in_specs=[pl.BlockSpec(memory_space=pltpu.VMEM)] * 3,
        out_specs=(pl.BlockSpec(memory_space=pltpu.VMEM),) * 2,
        scratch_shapes=[
            pltpu.VMEM((2, EZ, EX, 128), jnp.float32),
            pltpu.VMEM((2, EZ, EX, 128), jnp.float32),
            *([pltpu.VMEM((FINE_SWEEPS, EZ, EX, 128), jnp.float32)] * 4),
            *([fine] * 10),
            pltpu.VMEM((2, 9, NZ, 128), jnp.float32),
            pltpu.VMEM((2, 9, NZ, 128), jnp.float32),
            pltpu.VMEM((2, 4, EX, 128), jnp.float32),
            pltpu.VMEM((2, 4, EX, 128), jnp.float32),
            pltpu.VMEM((5, CZ * CX, 128), jnp.float32),
            pltpu.VMEM((4, KZ, KX + 8, 128), jnp.float32),
            pltpu.VMEM((KZ, KX + 8, 128), jnp.float32),
            pltpu.VMEM((KZ, KX + 8, 128), jnp.float32),
            pltpu.VMEM((COARSE_SWEEPS, KZ, KX + 8, 128), jnp.float32),
            pltpu.VMEM((COARSE_SWEEPS, KZ, KX + 8, 128), jnp.float32),
            pltpu.VMEM((5, CZ, CX, 128), jnp.float32),
            pltpu.VMEM((2, 5, CZ, CX, 128), jnp.float32),
            pltpu.VMEM((CZ, CX, 128), jnp.float32),
            pltpu.SemaphoreType.DMA((18,)),
            pltpu.SemaphoreType.DMA((18,)),
        ],
        compiler_params=pltpu.CompilerParams(
            collective_id=0, has_side_effects=True, vmem_limit_bytes=40 << 20
        ),
        name="vcycle",
    )(right_side, phase, density_scale)


def solution(mesh):
    placed = P("gz", "xy", None, None)
    return jax.shard_map(
        body,
        mesh=mesh,
        in_specs=(placed, placed, placed),
        out_specs=(placed, placed),
        check_vma=False,
    )
```

```python
import jax
import jax.numpy as jnp
from jax import lax
from jax.experimental import pallas as pl
from jax.experimental.pallas import tpu as pltpu
from jax.sharding import PartitionSpec as P

PY = 8
FINE_SWEEPS = 4
COARSE_SWEEPS = 8

NZ, BX, BY = 16, 32, 128
HZ = 5
EZ, EX = NZ + 2 * HZ, BX + 16
X0 = 8
CZ, CX, CY = 8, 16, 64
KZ, KX = CZ + 16, CX + 16
AROUND = [(z, x, y) for z in (-1, 0, 1) for x in (-1, 0, 1) for y in (-1, 0, 1) if z or x or y]
EDGES = [(-1, -1), (-1, 1), (1, -1), (1, 1)]
EDGE_ROWS = [(f, j, i) for f in (0, 1) for j in range(1, 5) for i in range(1, 6 - f - j)]


def chebyshev_table(low_bound, sweeps):
    middle = 0.5 * (2.0 + low_bound)
    radius = 0.5 * (2.0 - low_bound)
    quotient = middle / radius
    previous = 1.0 / quotient
    coeffs = []
    for number in range(sweeps):
        current = 1.0 / (2.0 * quotient - previous)
        coeffs.append((current * previous, 2.0 * current / radius))
        previous = current
    return (1.0 / middle, coeffs)


def lanes_of(rows):
    return lax.broadcasted_iota(jnp.int32, (rows, 128), 1)


def face(total):
    return 2.0 / jnp.maximum(total, 1e-3)


def kernel(
    right_ref, phase_ref, scale_ref, out_ref, coarse_ref,
    e0, e1, s0, s1, r0, r1, fz0, fz1, fx0, fx1, fy0, fy1, gy0, gy1, ig0, ig1,
    xsend, xrecv, esend, erecv, pack, unpack, stage,
    cp, cpack, cps, crp, rpack, crs, cs, cr, ci, sx, rx, cx,
    send_sem, recv_sem,
):
    b = lax.axis_index("xy")
    g = lax.axis_index("gz")
    row, col = b // PY, b % PY
    n_rows = lax.axis_size("xy") // PY
    n_gz = lax.axis_size("gz")
    there = ((g > 0, g < n_gz - 1), (row > 0, row < n_rows - 1), (col > 0, col < PY - 1))

    def exists(d):
        found = None
        for axis in (0, 1, 2):
            if d[axis]:
                flag = there[axis][1 if d[axis] > 0 else 0]
                found = flag if found is None else found & flag
        return found

    def device(d):
        return {"xy": b + PY * d[1] + d[2], "gz": g + d[0]}

    sent = []

    def message(number, d, source, target):
        copy = pltpu.make_async_remote_copy(
            src_ref=source, dst_ref=target,
            send_sem=send_sem.at[number], recv_sem=recv_sem.at[number],
            device_id=device(d), device_id_type=pl.DeviceIdType.MESH,
        )
        back = tuple(-v for v in d)
        sent.append((d, copy))
        pl.when(exists(d))(copy.start)
        return lambda: pl.when(exists(back))(copy.wait_recv)

    for f in (0, 1):
        for p in range(EZ):
            if HZ <= p < HZ + NZ:
                e0[f, p, 0:X0] = jnp.zeros((X0, 128), jnp.float32)
                e0[f, p, X0 + BX:EX] = jnp.zeros((EX - X0 - BX, 128), jnp.float32)
            else:
                e0[f, p] = jnp.zeros((EX, 128), jnp.float32)
    for side in (0, 1):
        for a in range(4):
            unpack[side, a] = jnp.zeros((EX, 128), jnp.float32)

    barrier = pltpu.get_barrier_semaphore()
    count = jnp.int32(0)
    for d in AROUND:
        count = count + exists(d).astype(jnp.int32)

        @pl.when(exists(d))
        def _():
            pl.semaphore_signal(barrier, inc=1, device_id=device(d), device_id_type=pl.DeviceIdType.MESH)

    for z in range(NZ):
        heavy = jnp.where(phase_ref[z, 0] == 1, 1000.0, 1.0).astype(jnp.float32)
        e0[0, HZ + z, X0:X0 + BX] = heavy * scale_ref[z, 0]
        e0[1, HZ + z, X0:X0 + BX] = right_ref[z, 0]

    for p in range(KZ):
        for f in (0, 1):
            cp[f, p] = jnp.zeros((KX, 128), jnp.float32)
        for side in (0, 1):
            if p < 6:
                cps[side, p] = jnp.zeros((KX, 128), jnp.float32)
            if p < 3:
                crs[side, p] = jnp.zeros((KX, 128), jnp.float32)
        if p < 12:
            crp[p] = jnp.zeros((KX, 128), jnp.float32)

    for j in range(9):
        f, at = (0, j) if j < 5 else (1, j - 5)
        width = 5 - f
        xsend[0, j] = e0[f, HZ:HZ + NZ, X0 + at, :]
        xsend[1, j] = e0[f, HZ:HZ + NZ, X0 + BX - width + at, :]

    for q, (dz, dx) in enumerate(EDGES):
        for n, (f, j, i) in enumerate(EDGE_ROWS):
            p = HZ + NZ - j if dz > 0 else HZ + j - 1
            r = X0 + BX - i if dx > 0 else X0 + i - 1
            esend[q, n:n + 1] = e0[f, p, r:r + 1, :]

    lane = lanes_of(BX)

    for a in (0, 1):
        packed = [None, None]
        for i in range(8):
            for f in (0, 1):
                v = e0[f, HZ + 8 * a + i, X0:X0 + BX]
                at = 16 * i + 8 * f
                for side in (0, 1):
                    rolled = pltpu.roll(v, (at + 8 * side) % 128, 1)
                    packed[side] = rolled if packed[side] is None else jnp.where(lane < at, packed[side], rolled)
        pack[0, a], pack[1, a] = packed

    pl.semaphore_wait(barrier, count)

    waits = []
    order = sorted(range(26), key=lambda n: (-abs(AROUND[n][1]), abs(AROUND[n][0]) + abs(AROUND[n][2])))
    for n in order:
        d = dz, dx, dy = AROUND[n]
        if dy:
            side = (dy + 1) // 2
            size = 1 if dz else 2
            from_group, to_group = {1: (1, 0), -1: (0, 3), 0: (0, 1)}[dz]
            from_row, rows = {1: (BX - 8, 8), -1: (0, 8), 0: (0, BX)}[dx]
            to_row = {1: 0, -1: X0 + BX, 0: X0}[dx]
            source = pack.at[side, pl.ds(from_group, size), pl.ds(from_row, rows)]
            target = unpack.at[side, pl.ds(to_group, size), pl.ds(to_row, rows)]
        elif dz and dx:
            q = EDGES.index((dz, dx))
            source, target = esend.at[q], erecv.at[q]
        elif dx:
            source, target = xsend.at[(dx + 1) // 2], xrecv.at[(dx + 1) // 2]
        else:
            source = e0.at[:, pl.ds(NZ if dz > 0 else HZ, HZ), pl.ds(X0, BX)]
            target = e0.at[:, pl.ds(0 if dz > 0 else HZ + NZ, HZ), pl.ds(X0, BX)]
        waits.append(message(n, d, source, target))
    for wait in waits:
        wait()

    for side in (0, 1):
        @pl.when(there[1][1 - side])
        def _():
            for j in range(9):
                f, at = (0, j) if j < 5 else (1, j - 5)
                width = 5 - f
                to = X0 + BX + at if side == 0 else X0 - width + at
                e0[f, HZ:HZ + NZ, to, :] = xrecv[side, j]

    for q, (dz, dx) in enumerate(EDGES):
        @pl.when(exists((-dz, -dx, 0)))
        def _():
            for n, (f, j, i) in enumerate(EDGE_ROWS):
                p = HZ - j if dz > 0 else HZ + NZ + j - 1
                r = X0 - i if dx > 0 else X0 + BX + i - 1
                e0[f, p, r:r + 1, :] = erecv[q, n:n + 1]

    lane = lanes_of(EX)
    for a in range(4):
        right, left = unpack[0, a], unpack[1, a]
        for i in range(8):
            p = i - 3 if a == 0 else HZ + 8 * (a - 1) + i
            if not 0 <= p < EZ:
                continue
            for f in (0, 1):
                at = 16 * i + 8 * f
                low = pltpu.roll(right, (128 - at) % 128, 1)
                high = pltpu.roll(left, (120 - at) % 128, 1)
                e1[f, p] = jnp.where(lane < 8, low, jnp.where(lane >= 120, high, 0.0))

    lane8 = lanes_of(8)

    def y_low(v):
        a0, a1 = pltpu.roll(v[0], 1, 1), pltpu.roll(v[1], 1, 1)
        return jnp.where(lane8 == 0, a1, a0), jnp.where(lane8 == 0, a0, a1)

    def y_high(v):
        a0, a1 = pltpu.roll(v[0], 127, 1), pltpu.roll(v[1], 127, 1)
        return jnp.where(lane8 == 127, a1, a0), jnp.where(lane8 == 127, a0, a1)

    center, coeffs = chebyshev_table(0.5, FINE_SWEEPS)
    es, fzs, fxs, fys, gys, igs = (e0, e1), (fz0, fz1), (fx0, fx1), (fy0, fy1), (gy0, gy1), (ig0, ig1)

    def at_rows(refs, p, r, *lead):
        return [ref[(*lead, p, pl.ds(r, 8))] for ref in refs]

    tiles = [4 + 8 * i for i in range(5)]

    def faces_step(p, below):
        out = []
        for i, r in enumerate(tiles):
            d = at_rows(es, p, r, 0)
            above = at_rows(es, p + 1, r, 0)
            before = at_rows(es, p, r - 1, 0)
            after = at_rows(es, p, r + 1, 0)
            left, right = y_low(d), y_high(d)
            for t in (0, 1):
                up = face(d[t] + above[t])
                w, e = face(d[t] + before[t]), face(d[t] + after[t])
                v, h = face(d[t] + left[t]), face(d[t] + right[t])
                inverse = jnp.where(d[t] > 0.0, 1.0 / (below[2 * i + t] + up + w + e + v + h), 0.0)
                fzs[t][p + 1, pl.ds(r, 8)] = up
                fxs[t][p, pl.ds(r, 8)] = w
                if r == tiles[-1]:
                    fxs[t][p, pl.ds(r + 1, 8)] = e
                fys[t][p, pl.ds(r, 8)] = v
                gys[t][p, pl.ds(r, 8)] = h
                igs[t][p, pl.ds(r, 8)] = inverse
                ss[t][0, p, pl.ds(r, 8)] = es[t][1, p, pl.ds(r, 8)] * inverse * center
                out.append(up)
        return tuple(out)

    ss, rs = (s0, s1), (r0, r1)
    below = []
    for r in tiles:
        d, above = at_rows(es, 0, r, 0), at_rows(es, 1, r, 0)
        for t in (0, 1):
            up = face(d[t] + above[t])
            fzs[t][1, pl.ds(r, 8)] = up
            below.append(up)
    lax.fori_loop(1, EZ - 1, faces_step, tuple(below))

    dot_kw = dict(preferred_element_type=jnp.float32, precision=lax.Precision.HIGHEST)
    from_lane = lax.broadcasted_iota(jnp.int32, (128, 128), 0)
    to_lane = lax.broadcasted_iota(jnp.int32, (128, 128), 1)
    def ones(mask):
        return jnp.where(mask, 1.0, 0.0).astype(jnp.float32)

    pairs = (ones(from_lane // 2 == to_lane), ones(from_lane // 2 == to_lane - CY))
    evens = (ones(from_lane == 2 * to_lane), ones(from_lane == 2 * to_lane - 2 * CY))
    both = evens[0] + jnp.where((from_lane == 2 * to_lane + 2) & (to_lane < CY), 1.0, 0.0).astype(jnp.float32)

    def row_pairs(ref, p):
        return ref[p, pl.ds(X0, CX, stride=2), :] + ref[p, pl.ds(X0 + 1, CX, stride=2), :]

    for c in range(CZ):
        p = HZ + 2 * c
        rows = pl.ds(c * CX, CX)
        low_z, high_z = row_pairs(fz0, p), row_pairs(fz0, p + 2)
        low_x = fx0[p, pl.ds(X0, CX, stride=2), :] + fx0[p + 1, pl.ds(X0, CX, stride=2), :]
        high_x = fx0[p, pl.ds(X0 + 2, CX, stride=2), :] + fx0[p + 1, pl.ds(X0 + 2, CX, stride=2), :]
        stage[0, rows] = low_z
        stage[1, rows] = low_x
        stage[2, rows] = low_z + high_z + low_x + high_x
        stage[3, rows] = row_pairs(fy0, p) + row_pairs(fy0, p + 1)
        stage[4, rows] = row_pairs(fy1, p) + row_pairs(fy1, p + 1)

    wide = lanes_of(CZ * CX)
    last = jnp.where(wide == CY - 1, pltpu.roll(stage[4], CY - 1, 1), 0.0)
    first_pair = jnp.dot(stage[2], pairs[0], **dot_kw) + jnp.dot(stage[3], both, **dot_kw) + last
    first_pair = first_pair + jnp.dot(stage[0], pairs[1], **dot_kw)
    second_pair = jnp.dot(stage[1], pairs[0], **dot_kw) + jnp.dot(stage[3], evens[1], **dot_kw)
    fields = [(v * 0.0625).reshape(CZ, CX, 128) for v in (first_pair, second_pair)]
    cp[0, 8:8 + CZ, 8:8 + CX], cp[1, 8:8 + CZ, 8:8 + CX] = fields
    clane = lanes_of(CX)
    for a in (0, 1):
        packed = [None, None]
        for i in range(4):
            for f in range(4):
                at = 32 * i + 8 * f
                for side in (0, 1):
                    shift = (at - 64 * (f % 2) - 56 * side) % 128
                    rolled = pltpu.roll(fields[f // 2][4 * a + i], shift, 1)
                    packed[side] = rolled if packed[side] is None else jnp.where(clane < at, packed[side], rolled)
        cpack[0, a], cpack[1, a] = packed

    def coarse_messages(number, depth, array, strips_from, strips_to):
        lead = (slice(None),) if len(array.shape) == 4 else ()
        groups = strips_from.shape[1]
        waits = []
        for n in order:
            d = dz, dx, dy = AROUND[n]
            from_row, to_row, rows = {1: (8, 0, 8), -1: (0, 24, 8), 0: (0, 8, CX)}[dx]
            block = {1: 0, -1: 2, 0: 1}[dz]
            if dy:
                side = (dy + 1) // 2
                source = strips_from.at[side, :, pl.ds(from_row, rows)]
                target = strips_to.at[side, pl.ds(groups * block, groups), pl.ds(to_row, rows)]
            else:
                source = array.at[(*lead, pl.ds(depth, depth), pl.ds(8 + from_row, rows))]
                target = array.at[(*lead, pl.ds(depth * block, depth), pl.ds(to_row, rows))]
            waits.append(message(number + n, d, source, target))
        return waits

    face_waits = coarse_messages(26, CZ, cp, cpack, cps)

    def sweep(k):
        first, end = 2 + k, EZ - 2 - k
        keep, push = coeffs[k]
        rows_of = tiles if k + 1 < FINE_SWEEPS else [X0 + 8 * i for i in range(4)]
        lanes = (0, 1) if k + 1 < FINE_SWEEPS else (0,)
        source = (lambda t, p, r: es[t][1, p, pl.ds(r, 8)]) if k == 0 else (lambda t, p, r: rs[t][k - 1, p, pl.ds(r, 8)])

        def step(j, fluxes):
            fluxes = list(fluxes)
            for i, r in enumerate(rows_of):
                for u in (0, 1):
                    p = first + 2 * j + u
                    c = at_rows(ss, p, r, k)
                    left, right = y_low(c), y_high(c)
                    for t in lanes:
                        up = fzs[t][p + 1, pl.ds(r, 8)] * (ss[t][k, p + 1, pl.ds(r, 8)] - c[t])
                        total = fluxes[len(lanes) * i + t] - up
                        total = total + fxs[t][p, pl.ds(r, 8)] * (c[t] - ss[t][k, p, pl.ds(r - 1, 8)])
                        total = total + fxs[t][p, pl.ds(r + 1, 8)] * (c[t] - ss[t][k, p, pl.ds(r + 1, 8)])
                        total = total + fys[t][p, pl.ds(r, 8)] * (c[t] - left[t])
                        total = total + gys[t][p, pl.ds(r, 8)] * (c[t] - right[t])
                        residual = source(t, p, r) - total
                        rs[t][k, p, pl.ds(r, 8)] = residual
                        if k + 1 < FINE_SWEEPS:
                            ss[t][k + 1, p, pl.ds(r, 8)] = keep * c[t] + (push * residual) * igs[t][p, pl.ds(r, 8)]
                        fluxes[len(lanes) * i + t] = up
            return tuple(fluxes)

        fluxes = []
        for r in rows_of:
            for t in lanes:
                fluxes.append(
                    fzs[t][first, pl.ds(r, 8)] * (ss[t][k, first, pl.ds(r, 8)] - ss[t][k, first - 1, pl.ds(r, 8)])
                )
        lax.fori_loop(0, (end - first) // 2, step, tuple(fluxes))

    for k in range(FINE_SWEEPS):
        sweep(k)

    last_residual = rs[0].at[FINE_SWEEPS - 1]
    for c in range(CZ):
        p = HZ + 2 * c
        stage[0, pl.ds(c * CX, CX)] = row_pairs(last_residual, p) + row_pairs(last_residual, p + 1)
    half = CZ * CX // 2
    planes = jnp.dot(stage[0, 0:half], pairs[0], **dot_kw) + jnp.dot(stage[0, half:2 * half], pairs[1], **dot_kw)
    planes = (planes * 0.125).reshape(CZ // 2, CX, 128)
    crp[4:8, 8:8 + CX] = planes
    packed = [None, None]
    for z in range(CZ):
        for side in (0, 1):
            rolled = pltpu.roll(planes[z % 4], (8 * z - 64 * (z // 4) - 56 * side) % 128, 1)
            packed[side] = rolled if packed[side] is None else jnp.where(clane < 8 * z, packed[side], rolled)
    rpack[0, 0], rpack[1, 0] = packed
    right_waits = coarse_messages(52, CZ // 2, crp, rpack, crs)

    xlane = lanes_of(KX)

    def widen(base, second, right, left, at):
        base = pltpu.roll(base, 64, 1) if second else base
        right = pltpu.roll(right, (64 - at) % 128, 1)
        left = pltpu.roll(left, (120 - at) % 128, 1)
        return jnp.where(xlane < CY, base, jnp.where(xlane < 96, right, left))

    for wait in face_waits:
        wait()
    for p in range(KZ):
        for f in range(4):
            cs[f, p, 0:KX] = widen(
                cp[f // 2, p], f % 2, cps[0, p // 4], cps[1, p // 4], 32 * (p % 4) + 8 * f
            )
        diagonal = cs[0, p, 0:KX]
        ci[p, 0:KX] = jnp.where(diagonal > 0.0, 1.0 / diagonal, 0.0)

    for wait in right_waits:
        wait()
    center, ccoeffs = chebyshev_table(0.1, COARSE_SWEEPS)
    for p in range(KZ):
        z = p % 8
        value = widen(crp[4 * (p // 8) + z % 4], z // 4, crs[0, p // 8], crs[1, p // 8], 8 * z)
        cr[p, 0:KX] = value
        sx[0, p, 0:KX] = value * ci[p, 0:KX] * center

    def coarse_sweep(k):
        halo = COARSE_SWEEPS - 2 - k
        first, count = 8 - halo, CZ + 2 * halo
        n_tiles = (CX + 2 * halo + 7) // 8
        r_first = min(8 - halo, KX + 7 - 8 * n_tiles)
        rows_of = [r_first + 8 * i for i in range(n_tiles)]
        keep, push = ccoeffs[k]
        unroll = 4 if count % 4 == 0 else 2

        def step(j, fluxes):
            fluxes = list(fluxes)
            for i, r in enumerate(rows_of):
                rows = pl.ds(r, 8)
                for u in range(unroll):
                    p = first + unroll * j + u
                    c = sx[k, p, rows]
                    above = sx[k, p + 1, rows]
                    fz = cs[1, p + 1, rows]
                    fy = cs[3, p, rows]
                    total = cs[0, p, rows] * c - fluxes[i] - fz * above
                    total = total - cs[2, p, rows] * sx[k, p, pl.ds(r - 1, 8)]
                    total = total - cs[2, p, pl.ds(r + 1, 8)] * sx[k, p, pl.ds(r + 1, 8)]
                    total = total - fy * pltpu.roll(c, 1, 1) - pltpu.roll(fy * c, 127, 1)
                    residual = (cr if k == 0 else rx.at[k])[p, rows] - total
                    if k + 2 < COARSE_SWEEPS:
                        rx[k + 1, p, rows] = residual
                    sx[k + 1, p, rows] = keep * c + (push * residual) * ci[p, rows]
                    fluxes[i] = fz * c
            return tuple(fluxes)

        lax.fori_loop(
            0, count // unroll, step,
            tuple(cs[1, first, pl.ds(r, 8)] * sx[k, first - 1, pl.ds(r, 8)] for r in rows_of),
        )

    for k in range(COARSE_SWEEPS - 1):
        coarse_sweep(k)
    for z in range(CZ):
        mine = sx[0, 8 + z, 8:8 + CX]
        for k in range(1, COARSE_SWEEPS):
            mine = mine + sx[k, 8 + z, 8:8 + CX]
        cx[z] = jnp.where(clane < CY, mine, 0.0)

    spread = jnp.where(to_lane // 2 == from_lane, 1.0, 0.0).astype(jnp.float32)
    stage[1] = jnp.dot(cx[...].reshape(CZ * CX, 128), spread, **dot_kw)

    for c in range(CZ):
        coarse_ref[c, 0] = cx[c, :, 0:CY]
        wide_rows = stage[1, pl.ds(c * CX, CX), :]
        spot = pl.ds(BX * (c % 2), CX, stride=2), pl.ds(BX * (c % 2) + 1, CX, stride=2)
        stage[2, spot[0], :] = wide_rows
        stage[2, spot[1], :] = wide_rows
        twice = stage[2, pl.ds(BX * (c % 2), BX), :]
        for i in (0, 1):
            mine = s0[0, HZ + 2 * c + i, X0:X0 + BX]
            for k in range(1, FINE_SWEEPS):
                mine = mine + s0[k, HZ + 2 * c + i, X0:X0 + BX]
            out_ref[2 * c + i, 0] = mine + twice

    for d, copy in sent:
        pl.when(exists(d))(copy.wait_send)


def body(right_side, phase, density_scale):
    fine = pltpu.VMEM((EZ, EX, 128), jnp.float32)
    return pl.pallas_call(
        kernel,
        out_shape=(
            jax.ShapeDtypeStruct((NZ, 1, BX, BY), jnp.float32),
            jax.ShapeDtypeStruct((CZ, 1, CX, CY), jnp.float32),
        ),
        in_specs=[pl.BlockSpec(memory_space=pltpu.VMEM)] * 3,
        out_specs=(pl.BlockSpec(memory_space=pltpu.VMEM),) * 2,
        scratch_shapes=[
            pltpu.VMEM((2, EZ, EX, 128), jnp.float32),
            pltpu.VMEM((2, EZ, EX, 128), jnp.float32),
            *([pltpu.VMEM((FINE_SWEEPS, EZ, EX, 128), jnp.float32)] * 4),
            *([fine] * 10),
            pltpu.VMEM((2, 9, NZ, 128), jnp.float32),
            pltpu.VMEM((2, 9, NZ, 128), jnp.float32),
            pltpu.VMEM((4, 16, 128), jnp.float32),
            pltpu.VMEM((4, 16, 128), jnp.float32),
            pltpu.VMEM((2, 2, BX, 128), jnp.float32),
            pltpu.VMEM((2, 4, EX, 128), jnp.float32),
            pltpu.VMEM((5, CZ * CX, 128), jnp.float32),
            pltpu.VMEM((2, KZ, KX, 128), jnp.float32),
            pltpu.VMEM((2, 2, CX, 128), jnp.float32),
            pltpu.VMEM((2, 6, KX, 128), jnp.float32),
            pltpu.VMEM((12, KX, 128), jnp.float32),
            pltpu.VMEM((2, 1, CX, 128), jnp.float32),
            pltpu.VMEM((2, 3, KX, 128), jnp.float32),
            pltpu.VMEM((4, KZ, KX + 8, 128), jnp.float32),
            pltpu.VMEM((KZ, KX + 8, 128), jnp.float32),
            pltpu.VMEM((KZ, KX + 8, 128), jnp.float32),
            pltpu.VMEM((COARSE_SWEEPS, KZ, KX + 8, 128), jnp.float32),
            pltpu.VMEM((COARSE_SWEEPS, KZ, KX + 8, 128), jnp.float32),
            pltpu.VMEM((CZ, CX, 128), jnp.float32),
            pltpu.SemaphoreType.DMA((78,)),
            pltpu.SemaphoreType.DMA((78,)),
        ],
        compiler_params=pltpu.CompilerParams(
            collective_id=0, has_side_effects=True, vmem_limit_bytes=40 << 20
        ),
        name="vcycle",
    )(right_side, phase, density_scale)


def solution(mesh):
    placed = P("gz", "xy", None, None)
    return jax.shard_map(
        body,
        mesh=mesh,
        in_specs=(placed, placed, placed),
        out_specs=(placed, placed),
        check_vma=False,
    )
```

```python
import jax
import jax.numpy as jnp
from jax import lax
from jax.experimental import pallas as pl
from jax.experimental.pallas import tpu as pltpu
from jax.sharding import PartitionSpec as P

PY = 8
FINE_SWEEPS = 4
COARSE_SWEEPS = 8

NZ, BX, BY = 16, 32, 128
HZ = 5
EZ, EX = NZ + 2 * HZ, BX + 16
X0 = 8
CZ, CX, CY = 8, 16, 64
KZ, KX = CZ + 16, CX + 16
AROUND = [(z, x, y) for z in (-1, 0, 1) for x in (-1, 0, 1) for y in (-1, 0, 1) if z or x or y]
EDGES = [(-1, -1), (-1, 1), (1, -1), (1, 1)]
X_ROWS = [(0, i) for i in range(5)] + [(1, i) for i in range(4)]
EDGE_ROWS = [(f, j, i) for f in (0, 1) for j in range(1, 5) for i in range(1, 6 - f - j)]


def chebyshev_table(low_bound, sweeps):
    middle = 0.5 * (2.0 + low_bound)
    radius = 0.5 * (2.0 - low_bound)
    quotient = middle / radius
    previous = 1.0 / quotient
    coeffs = []
    for number in range(sweeps):
        current = 1.0 / (2.0 * quotient - previous)
        coeffs.append((current * previous, 2.0 * current / radius))
        previous = current
    return (1.0 / middle, coeffs)


def lanes_of(rows):
    return lax.broadcasted_iota(jnp.int32, (rows, 128), 1)


def face(total):
    return 2.0 / jnp.maximum(total, 1e-3)


def kernel(
    right_ref, phase_ref, scale_ref, out_ref, coarse_ref, phase, scale,
    e0, e1, s0, s1, r0, r1, fz0, fz1, fx0, fx1, fy0, fy1, gy0, gy1, ig0, ig1,
    xsend, xrecv, esend, erecv, pack, unpack, stage,
    cp, cpack, cps, crp, rpack, crs, cs, cr, ci, sx, rx, cx,
    fetch_sem, send_sem, recv_sem,
):
    b = lax.axis_index("xy")
    g = lax.axis_index("gz")
    row, col = b // PY, b % PY
    n_rows = lax.axis_size("xy") // PY
    n_gz = lax.axis_size("gz")
    there = ((g > 0, g < n_gz - 1), (row > 0, row < n_rows - 1), (col > 0, col < PY - 1))

    def exists(d):
        found = None
        for axis in (0, 1, 2):
            if d[axis]:
                flag = there[axis][1 if d[axis] > 0 else 0]
                found = flag if found is None else found & flag
        return found

    def device(d):
        return {"xy": b + PY * d[1] + d[2], "gz": g + d[0]}

    sent = []

    def message(number, d, source, target):
        copy = pltpu.make_async_remote_copy(
            src_ref=source, dst_ref=target,
            send_sem=send_sem.at[number], recv_sem=recv_sem.at[number],
            device_id=device(d), device_id_type=pl.DeviceIdType.MESH,
        )
        back = tuple(-v for v in d)
        sent.append((d, copy))
        pl.when(exists(d))(copy.start)
        return lambda: pl.when(exists(back))(copy.wait_recv)

    barrier = pltpu.get_barrier_semaphore()
    count = jnp.int32(0)
    for d in AROUND:
        count = count + exists(d).astype(jnp.int32)

        @pl.when(exists(d))
        def _():
            pl.semaphore_signal(barrier, inc=1, device_id=device(d), device_id_type=pl.DeviceIdType.MESH)

    fetched = [
        pltpu.make_async_copy(source, target, fetch_sem.at[n])
        for n, (source, target) in enumerate((
            (phase_ref.at[:, 0], phase), (scale_ref.at[:, 0], scale),
            (right_ref.at[:, 0], e0.at[1, pl.ds(HZ, NZ), pl.ds(X0, BX)]),
        ))
    ]
    for copy in fetched:
        copy.start()

    def clear(ref, *at):
        ref[at] = jnp.zeros(ref.at[at].shape, jnp.float32)

    def clear_without(d, ref, *at):
        @pl.when(jnp.logical_not(exists(d)))
        def _():
            clear(ref, *at)

    for f in (0, 1):
        for p in range(EZ):
            clear(e0, f, p, slice(0, X0))
            clear(e0, f, p, slice(X0 + BX, EX))
            if p < HZ or p >= HZ + NZ:
                clear_without((-1 if p < HZ else 1, 0, 0), e0, f, p, slice(X0, X0 + BX))
    for d in AROUND:
        dz, dx, dy = d
        if dy:
            groups = {-1: (0,), 0: (1, 2), 1: (3,)}[dz]
            rows = {-1: slice(0, X0), 0: slice(X0, X0 + BX), 1: slice(X0 + BX, EX)}[dx]
            for a in groups:
                clear_without(d, unpack, 0 if dy > 0 else 1, a, rows)

    for copy in fetched:
        copy.wait()
    for z in range(NZ):
        heavy = jnp.where(phase[z] == 1, 1000.0, 1.0).astype(jnp.float32)
        e0[0, HZ + z, X0:X0 + BX] = heavy * scale[z]

    for j, (f, away) in enumerate(X_ROWS):
        xsend[0, j] = e0[f, HZ:HZ + NZ, X0 + away, :]
        xsend[1, j] = e0[f, HZ:HZ + NZ, X0 + BX - 1 - away, :]

    for q, (dz, dx) in enumerate(EDGES):
        for n, (f, j, i) in enumerate(EDGE_ROWS):
            p = HZ + NZ - j if dz > 0 else HZ + j - 1
            r = X0 + BX - i if dx > 0 else X0 + i - 1
            esend[q, n:n + 1] = e0[f, p, r:r + 1, :]

    lane = lanes_of(BX)

    for a in (0, 1):
        packed = [None, None]
        for i in range(8):
            for f in (0, 1):
                v = e0[f, HZ + 8 * a + i, X0:X0 + BX]
                at = 16 * i + 8 * f
                for side in (0, 1):
                    rolled = pltpu.roll(v, (at + 8 * side) % 128, 1)
                    packed[side] = rolled if packed[side] is None else jnp.where(lane < at, packed[side], rolled)
        pack[0, a], pack[1, a] = packed

    for p in range(KZ):
        for f in (0, 1):
            clear(cp, f, p)
        for side in (0, 1):
            if p < 6:
                clear(cps, side, p)
            if p < 3:
                clear(crs, side, p)
        if p < 12:
            clear(crp, p)

    pl.semaphore_wait(barrier, count)

    first_waits, waits = [], []
    order = sorted(range(26), key=lambda n: (-abs(AROUND[n][1]), abs(AROUND[n][0]) + abs(AROUND[n][2])))
    for n in order:
        d = dz, dx, dy = AROUND[n]
        if abs(dz) + abs(dx) + abs(dy) > 1:
            continue
        if dx:
            side = (dx + 1) // 2
            source, target = xsend.at[side, pl.ds(0, 1)], xrecv.at[side, pl.ds(0, 1)]
        elif dz:
            source = e0.at[0, HZ + NZ - 1 if dz > 0 else HZ, pl.ds(X0, BX)]
            target = e0.at[0, HZ - 1 if dz > 0 else HZ + NZ, pl.ds(X0, BX)]
        else:
            side = (dy + 1) // 2
            source, target = pack.at[side], unpack.at[side, pl.ds(1, 2), pl.ds(X0, BX)]
        first_waits.append(message(n, d, source, target))
    for n in order:
        d = dz, dx, dy = AROUND[n]
        if dy and (dz or dx):
            side = (dy + 1) // 2
            size = 1 if dz else 2
            from_group, to_group = {1: (1, 0), -1: (0, 3), 0: (0, 1)}[dz]
            from_row, rows = {1: (BX - 8, 8), -1: (0, 8), 0: (0, BX)}[dx]
            to_row = {1: 0, -1: X0 + BX, 0: X0}[dx]
            source = pack.at[side, pl.ds(from_group, size), pl.ds(from_row, rows)]
            target = unpack.at[side, pl.ds(to_group, size), pl.ds(to_row, rows)]
            waits.append(message(n, d, source, target))
        elif dz and dx:
            q = EDGES.index((dz, dx))
            waits.append(message(n, d, esend.at[q], erecv.at[q]))
        elif dx:
            side = (dx + 1) // 2
            waits.append(message(78 + side, d, xsend.at[side, pl.ds(1, 8)], xrecv.at[side, pl.ds(1, 8)]))
        elif dz:
            side = (dz + 1) // 2
            for f in (0, 1):
                if dz > 0:
                    source, target = HZ + NZ - 5 + f, f
                else:
                    source, target = HZ + 1 - f, HZ + NZ + 1 - f
                waits.append(message(
                    80 + 2 * f + side, d,
                    e0.at[f, pl.ds(source, 4), pl.ds(X0, BX)],
                    e0.at[f, pl.ds(target, 4), pl.ds(X0, BX)],
                ))

    def place_rows(numbers):
        for side in (0, 1):
            @pl.when(there[1][1 - side])
            def _():
                for j in numbers:
                    f, away = X_ROWS[j]
                    to = X0 + BX + away if side == 0 else X0 - 1 - away
                    e0[f, HZ:HZ + NZ, to, :] = xrecv[side, j]

    def unpack_plane(p, rows):
        a = (p + 3) // 8
        right, left = unpack[0, a, rows], unpack[1, a, rows]
        lane = lanes_of(right.shape[0])
        for f in (0, 1):
            at = 16 * ((p + 3) % 8) + 8 * f
            low = pltpu.roll(right, (128 - at) % 128, 1)
            high = pltpu.roll(left, (120 - at) % 128, 1)
            e1[f, p, rows] = jnp.where(lane < 8, low, jnp.where(lane >= 120, high, 0.0))

    for wait in first_waits:
        wait()
    place_rows([0])
    for p in range(HZ, HZ + NZ):
        unpack_plane(p, slice(X0, X0 + BX))

    lane8 = lanes_of(8)

    def y_low(v):
        a0, a1 = pltpu.roll(v[0], 1, 1), pltpu.roll(v[1], 1, 1)
        return jnp.where(lane8 == 0, a1, a0), jnp.where(lane8 == 0, a0, a1)

    def y_high(v):
        a0, a1 = pltpu.roll(v[0], 127, 1), pltpu.roll(v[1], 127, 1)
        return jnp.where(lane8 == 127, a1, a0), jnp.where(lane8 == 127, a0, a1)

    center, coeffs = chebyshev_table(0.5, FINE_SWEEPS)
    es, fzs, fxs, fys, gys, igs = (e0, e1), (fz0, fz1), (fx0, fx1), (fy0, fy1), (gy0, gy1), (ig0, ig1)

    def at_rows(refs, p, r, *lead):
        return [ref[(*lead, p, pl.ds(r, 8))] for ref in refs]

    tiles = [4 + 8 * i for i in range(5)]

    def plane_faces(p, below, rows_of, lanes):
        out = []
        for i, r in enumerate(rows_of):
            d = at_rows(es, p, r, 0)
            left, right = y_low(d), y_high(d)
            for k, t in enumerate(lanes):
                up = face(d[t] + es[t][0, p + 1, pl.ds(r, 8)])
                w, e = face(d[t] + es[t][0, p, pl.ds(r - 1, 8)]), face(d[t] + es[t][0, p, pl.ds(r + 1, 8)])
                v, h = face(d[t] + left[t]), face(d[t] + right[t])
                inverse = jnp.where(d[t] > 0.0, 1.0 / (below[len(lanes) * i + k] + up + w + e + v + h), 0.0)
                fzs[t][p + 1, pl.ds(r, 8)] = up
                fxs[t][p, pl.ds(r, 8)] = w
                if r == rows_of[-1]:
                    fxs[t][p, pl.ds(r + 1, 8)] = e
                fys[t][p, pl.ds(r, 8)] = v
                gys[t][p, pl.ds(r, 8)] = h
                igs[t][p, pl.ds(r, 8)] = inverse
                ss[t][0, p, pl.ds(r, 8)] = es[t][1, p, pl.ds(r, 8)] * inverse * center
                out.append(up)
        return tuple(out)

    def faces(first, end, rows_of, lanes):
        below = []
        for r in rows_of:
            for t in lanes:
                up = face(es[t][0, first - 1, pl.ds(r, 8)] + es[t][0, first, pl.ds(r, 8)])
                fzs[t][first, pl.ds(r, 8)] = up
                below.append(up)
        step = 2 if (end - first) % 2 == 0 else 1

        def some(j, below):
            for u in range(step):
                below = plane_faces(first + step * j + u, below, rows_of, lanes)
            return below

        lax.fori_loop(0, (end - first) // step, some, tuple(below))

    ss, rs = (s0, s1), (r0, r1)
    own_rows = [X0 + 8 * i for i in range(4)]
    faces(HZ, HZ + NZ, own_rows, (0,))

    dot_kw = dict(preferred_element_type=jnp.float32, precision=lax.Precision.HIGHEST)
    from_lane = lax.broadcasted_iota(jnp.int32, (128, 128), 0)
    to_lane = lax.broadcasted_iota(jnp.int32, (128, 128), 1)
    def ones(mask):
        return jnp.where(mask, 1.0, 0.0).astype(jnp.float32)

    pairs = (ones(from_lane // 2 == to_lane), ones(from_lane // 2 == to_lane - CY))
    evens = (ones(from_lane == 2 * to_lane), ones(from_lane == 2 * to_lane - 2 * CY))
    odds = ones(from_lane == 2 * to_lane + 1)

    def row_pairs(ref, p):
        return ref[p, pl.ds(X0, CX, stride=2), :] + ref[p, pl.ds(X0 + 1, CX, stride=2), :]

    for c in range(CZ):
        p = HZ + 2 * c
        rows = pl.ds(c * CX, CX)
        low_z, high_z = row_pairs(fz0, p), row_pairs(fz0, p + 2)
        low_x = fx0[p, pl.ds(X0, CX, stride=2), :] + fx0[p + 1, pl.ds(X0, CX, stride=2), :]
        high_x = fx0[p, pl.ds(X0 + 2, CX, stride=2), :] + fx0[p + 1, pl.ds(X0 + 2, CX, stride=2), :]
        stage[0, rows] = low_z
        stage[1, rows] = low_x
        stage[2, rows] = low_z + high_z + low_x + high_x
        stage[3, rows] = row_pairs(fy0, p) + row_pairs(fy0, p + 1)
        stage[4, rows] = row_pairs(gy0, p) + row_pairs(gy0, p + 1)

    first_pair = jnp.dot(stage[2], pairs[0], **dot_kw) + jnp.dot(stage[3], evens[0], **dot_kw)
    first_pair = first_pair + jnp.dot(stage[4], odds, **dot_kw)
    first_pair = first_pair + jnp.dot(stage[0], pairs[1], **dot_kw)
    second_pair = jnp.dot(stage[1], pairs[0], **dot_kw) + jnp.dot(stage[3], evens[1], **dot_kw)
    fields = [(v * 0.0625).reshape(CZ, CX, 128) for v in (first_pair, second_pair)]
    cp[0, 8:8 + CZ, 8:8 + CX], cp[1, 8:8 + CZ, 8:8 + CX] = fields
    clane = lanes_of(CX)
    for a in (0, 1):
        packed = [None, None]
        for i in range(4):
            for f in range(4):
                at = 32 * i + 8 * f
                for side in (0, 1):
                    shift = (at - 64 * (f % 2) - 56 * side) % 128
                    rolled = pltpu.roll(fields[f // 2][4 * a + i], shift, 1)
                    packed[side] = rolled if packed[side] is None else jnp.where(clane < at, packed[side], rolled)
        cpack[0, a], cpack[1, a] = packed

    def coarse_messages(number, depth, array, strips_from, strips_to):
        lead = (slice(None),) if len(array.shape) == 4 else ()
        groups = strips_from.shape[1]
        waits = []
        for n in order:
            d = dz, dx, dy = AROUND[n]
            from_row, to_row, rows = {1: (8, 0, 8), -1: (0, 24, 8), 0: (0, 8, CX)}[dx]
            block = {1: 0, -1: 2, 0: 1}[dz]
            if dy:
                side = (dy + 1) // 2
                source = strips_from.at[side, :, pl.ds(from_row, rows)]
                target = strips_to.at[side, pl.ds(groups * block, groups), pl.ds(to_row, rows)]
            else:
                source = array.at[(*lead, pl.ds(depth, depth), pl.ds(8 + from_row, rows))]
                target = array.at[(*lead, pl.ds(depth * block, depth), pl.ds(to_row, rows))]
            waits.append(message(number + n, d, source, target))
        return waits

    def along(number, axis, source_of, target_of):
        waits = []
        for side in (0, 1):
            d = tuple((2 * side - 1) if k == axis else 0 for k in range(3))
            waits.append(message(number + side, d, source_of(side), target_of(side)))
        return waits

    edge, halo = (8, 16), (24, 0)
    planes_own, groups_own = pl.ds(8, CZ), pl.ds(2, 2)
    y_waits = along(
        26, 2, lambda side: cpack.at[side], lambda side: cps.at[side, groups_own, pl.ds(8, CX)]
    )
    x_waits = along(
        28, 1, lambda side: cp.at[:, planes_own, pl.ds(edge[side], 8)],
        lambda side: cp.at[:, planes_own, pl.ds(halo[side], 8)],
    )
    face_waits = along(
        30, 0, lambda side: cp.at[:, planes_own, pl.ds(8, CX)],
        lambda side: cp.at[:, pl.ds((16, 0)[side], CZ), pl.ds(8, CX)],
    )
    for wait in y_waits:
        wait()
    x_waits += along(
        32, 1, lambda side: cps.at[:, groups_own, pl.ds(edge[side], 8)],
        lambda side: cps.at[:, groups_own, pl.ds(halo[side], 8)],
    )


    for wait in waits:
        wait()
    place_rows(range(1, 9))
    for q, (dz, dx) in enumerate(EDGES):
        @pl.when(exists((-dz, -dx, 0)))
        def _():
            for n, (f, j, i) in enumerate(EDGE_ROWS):
                p = HZ - j if dz > 0 else HZ + NZ + j - 1
                r = X0 - i if dx > 0 else X0 + BX + i - 1
                e0[f, p, r:r + 1, :] = erecv[q, n:n + 1]

    for p in range(EZ):
        if HZ <= p < HZ + NZ:
            unpack_plane(p, slice(0, X0))
            unpack_plane(p, slice(X0 + BX, EX))
        else:
            unpack_plane(p, slice(0, EX))
    faces(HZ, HZ + NZ, [4], (0,))
    faces(HZ, HZ + NZ, [36], (0,))
    faces(HZ, HZ + NZ, tiles, (1,))
    faces(1, HZ, tiles, (0, 1))
    faces(HZ + NZ, EZ - 1, tiles, (0, 1))

    def sweep(k):
        first, end = 2 + k, EZ - 2 - k
        keep, push = coeffs[k]
        rows_of = tiles if k + 1 < FINE_SWEEPS else [X0 + 8 * i for i in range(4)]
        lanes = (0, 1) if k + 1 < FINE_SWEEPS else (0,)
        source = (lambda t, p, r: es[t][1, p, pl.ds(r, 8)]) if k == 0 else (lambda t, p, r: rs[t][k - 1, p, pl.ds(r, 8)])

        def step(j, fluxes):
            fluxes = list(fluxes)
            for i, r in enumerate(rows_of):
                for u in (0, 1):
                    p = first + 2 * j + u
                    c = at_rows(ss, p, r, k)
                    left, right = y_low(c), y_high(c)
                    for t in lanes:
                        up = fzs[t][p + 1, pl.ds(r, 8)] * (ss[t][k, p + 1, pl.ds(r, 8)] - c[t])
                        total = fluxes[len(lanes) * i + t] - up
                        total = total + fxs[t][p, pl.ds(r, 8)] * (c[t] - ss[t][k, p, pl.ds(r - 1, 8)])
                        total = total + fxs[t][p, pl.ds(r + 1, 8)] * (c[t] - ss[t][k, p, pl.ds(r + 1, 8)])
                        total = total + fys[t][p, pl.ds(r, 8)] * (c[t] - left[t])
                        total = total + gys[t][p, pl.ds(r, 8)] * (c[t] - right[t])
                        residual = source(t, p, r) - total
                        rs[t][k, p, pl.ds(r, 8)] = residual
                        if k + 1 < FINE_SWEEPS:
                            ss[t][k + 1, p, pl.ds(r, 8)] = keep * c[t] + (push * residual) * igs[t][p, pl.ds(r, 8)]
                        fluxes[len(lanes) * i + t] = up
            return tuple(fluxes)

        fluxes = []
        for r in rows_of:
            for t in lanes:
                fluxes.append(
                    fzs[t][first, pl.ds(r, 8)] * (ss[t][k, first, pl.ds(r, 8)] - ss[t][k, first - 1, pl.ds(r, 8)])
                )
        lax.fori_loop(0, (end - first) // 2, step, tuple(fluxes))

    sweep(0)
    sweep(1)
    sweep(2)
    for wait in x_waits:
        wait()
    for n, r in ((34, 0), (36, 24)):
        face_waits += along(
            n, 0, lambda side: cp.at[:, planes_own, pl.ds(r, 8)],
            lambda side: cp.at[:, pl.ds((16, 0)[side], CZ), pl.ds(r, 8)],
        )
    face_waits += along(
        38, 0, lambda side: cps.at[:, groups_own], lambda side: cps.at[:, pl.ds((4, 0)[side], 2)]
    )
    sweep(3)

    last_residual = rs[0].at[FINE_SWEEPS - 1]
    for c in range(CZ):
        p = HZ + 2 * c
        stage[0, pl.ds(c * CX, CX)] = row_pairs(last_residual, p) + row_pairs(last_residual, p + 1)
    half = CZ * CX // 2
    planes = jnp.dot(stage[0, 0:half], pairs[0], **dot_kw) + jnp.dot(stage[0, half:2 * half], pairs[1], **dot_kw)
    planes = (planes * 0.125).reshape(CZ // 2, CX, 128)
    crp[4:8, 8:8 + CX] = planes
    packed = [None, None]
    for z in range(CZ):
        for side in (0, 1):
            rolled = pltpu.roll(planes[z % 4], (8 * z - 64 * (z // 4) - 56 * side) % 128, 1)
            packed[side] = rolled if packed[side] is None else jnp.where(clane < 8 * z, packed[side], rolled)
    rpack[0, 0], rpack[1, 0] = packed
    right_waits = coarse_messages(52, CZ // 2, crp, rpack, crs)

    xlane = lanes_of(KX)

    def widen(base, second, right, left, at):
        base = pltpu.roll(base, 64, 1) if second else base
        right = pltpu.roll(right, (64 - at) % 128, 1)
        left = pltpu.roll(left, (120 - at) % 128, 1)
        return jnp.where(xlane < CY, base, jnp.where(xlane < 96, right, left))

    for wait in face_waits:
        wait()
    for p in range(KZ):
        for f in range(4):
            cs[f, p, 0:KX] = widen(
                cp[f // 2, p], f % 2, cps[0, p // 4], cps[1, p // 4], 32 * (p % 4) + 8 * f
            )
        diagonal = cs[0, p, 0:KX]
        ci[p, 0:KX] = jnp.where(diagonal > 0.0, 1.0 / diagonal, 0.0)

    for wait in right_waits:
        wait()
    center, ccoeffs = chebyshev_table(0.1, COARSE_SWEEPS)
    for p in range(KZ):
        z = p % 8
        value = widen(crp[4 * (p // 8) + z % 4], z // 4, crs[0, p // 8], crs[1, p // 8], 8 * z)
        cr[p, 0:KX] = value
        sx[0, p, 0:KX] = value * ci[p, 0:KX] * center

    def coarse_sweep(k):
        halo = COARSE_SWEEPS - 2 - k
        first, count = 8 - halo, CZ + 2 * halo
        n_tiles = (CX + 2 * halo + 7) // 8
        r_first = min(8 - halo, KX + 7 - 8 * n_tiles)
        rows_of = [r_first + 8 * i for i in range(n_tiles)]
        keep, push = ccoeffs[k]
        unroll = 4 if count % 4 == 0 else 2

        def step(j, fluxes):
            fluxes = list(fluxes)
            for i, r in enumerate(rows_of):
                rows = pl.ds(r, 8)
                for u in range(unroll):
                    p = first + unroll * j + u
                    c = sx[k, p, rows]
                    above = sx[k, p + 1, rows]
                    fz = cs[1, p + 1, rows]
                    fy = cs[3, p, rows]
                    total = cs[0, p, rows] * c - fluxes[i] - fz * above
                    total = total - cs[2, p, rows] * sx[k, p, pl.ds(r - 1, 8)]
                    total = total - cs[2, p, pl.ds(r + 1, 8)] * sx[k, p, pl.ds(r + 1, 8)]
                    total = total - fy * pltpu.roll(c, 1, 1) - pltpu.roll(fy * c, 127, 1)
                    residual = (cr if k == 0 else rx.at[k])[p, rows] - total
                    if k + 2 < COARSE_SWEEPS:
                        rx[k + 1, p, rows] = residual
                    sx[k + 1, p, rows] = keep * c + (push * residual) * ci[p, rows]
                    fluxes[i] = fz * c
            return tuple(fluxes)

        lax.fori_loop(
            0, count // unroll, step,
            tuple(cs[1, first, pl.ds(r, 8)] * sx[k, first - 1, pl.ds(r, 8)] for r in rows_of),
        )

    for k in range(COARSE_SWEEPS - 1):
        coarse_sweep(k)
    for z in range(CZ):
        mine = sx[0, 8 + z, 8:8 + CX]
        for k in range(1, COARSE_SWEEPS):
            mine = mine + sx[k, 8 + z, 8:8 + CX]
        cx[z] = jnp.where(clane < CY, mine, 0.0)

    spread = jnp.where(to_lane // 2 == from_lane, 1.0, 0.0).astype(jnp.float32)
    stage[1] = jnp.dot(cx[...].reshape(CZ * CX, 128), spread, **dot_kw)

    for c in range(CZ):
        coarse_ref[c, 0] = cx[c, :, 0:CY]
        wide_rows = stage[1, pl.ds(c * CX, CX), :]
        spot = pl.ds(BX * (c % 2), CX, stride=2), pl.ds(BX * (c % 2) + 1, CX, stride=2)
        stage[2, spot[0], :] = wide_rows
        stage[2, spot[1], :] = wide_rows
        twice = stage[2, pl.ds(BX * (c % 2), BX), :]
        for i in (0, 1):
            mine = s0[0, HZ + 2 * c + i, X0:X0 + BX]
            for k in range(1, FINE_SWEEPS):
                mine = mine + s0[k, HZ + 2 * c + i, X0:X0 + BX]
            out_ref[2 * c + i, 0] = mine + twice

    for d, copy in sent:
        pl.when(exists(d))(copy.wait_send)


def body(right_side, phase, density_scale):
    fine = pltpu.VMEM((EZ, EX, 128), jnp.float32)
    return pl.pallas_call(
        kernel,
        out_shape=(
            jax.ShapeDtypeStruct((NZ, 1, BX, BY), jnp.float32),
            jax.ShapeDtypeStruct((CZ, 1, CX, CY), jnp.float32),
        ),
        in_specs=[pl.BlockSpec(memory_space=pltpu.HBM)] * 3,
        out_specs=(pl.BlockSpec(memory_space=pltpu.VMEM),) * 2,
        scratch_shapes=[
            pltpu.VMEM((NZ, BX, BY), jnp.int32),
            pltpu.VMEM((NZ, BX, BY), jnp.float32),
            pltpu.VMEM((2, EZ, EX, 128), jnp.float32),
            pltpu.VMEM((2, EZ, EX, 128), jnp.float32),
            *([pltpu.VMEM((FINE_SWEEPS, EZ, EX, 128), jnp.float32)] * 4),
            *([fine] * 10),
            pltpu.VMEM((2, 9, NZ, 128), jnp.float32),
            pltpu.VMEM((2, 9, NZ, 128), jnp.float32),
            pltpu.VMEM((4, 16, 128), jnp.float32),
            pltpu.VMEM((4, 16, 128), jnp.float32),
            pltpu.VMEM((2, 2, BX, 128), jnp.float32),
            pltpu.VMEM((2, 4, EX, 128), jnp.float32),
            pltpu.VMEM((5, CZ * CX, 128), jnp.float32),
            pltpu.VMEM((2, KZ, KX, 128), jnp.float32),
            pltpu.VMEM((2, 2, CX, 128), jnp.float32),
            pltpu.VMEM((2, 6, KX, 128), jnp.float32),
            pltpu.VMEM((12, KX, 128), jnp.float32),
            pltpu.VMEM((2, 1, CX, 128), jnp.float32),
            pltpu.VMEM((2, 3, KX, 128), jnp.float32),
            pltpu.VMEM((4, KZ, KX + 8, 128), jnp.float32),
            pltpu.VMEM((KZ, KX + 8, 128), jnp.float32),
            pltpu.VMEM((KZ, KX + 8, 128), jnp.float32),
            pltpu.VMEM((COARSE_SWEEPS, KZ, KX + 8, 128), jnp.float32),
            pltpu.VMEM((COARSE_SWEEPS, KZ, KX + 8, 128), jnp.float32),
            pltpu.VMEM((CZ, CX, 128), jnp.float32),
            pltpu.SemaphoreType.DMA((3,)),
            pltpu.SemaphoreType.DMA((84,)),
            pltpu.SemaphoreType.DMA((84,)),
        ],
        compiler_params=pltpu.CompilerParams(
            collective_id=0, has_side_effects=True, vmem_limit_bytes=107 << 19
        ),
        name="vcycle",
    )(right_side, phase, density_scale)


def solution(mesh):
    placed = P("gz", "xy", None, None)
    return jax.shard_map(
        body,
        mesh=mesh,
        in_specs=(placed, placed, placed),
        out_specs=(placed, placed),
        check_vma=False,
    )
```

```python
import jax
import jax.numpy as jnp
from jax import lax
from jax.experimental import pallas as pl
from jax.experimental.pallas import tpu as pltpu
from jax.sharding import PartitionSpec as P

PY = 8
FINE_SWEEPS = 4
COARSE_SWEEPS = 8

NZ, BX, BY = 16, 32, 128
HZ = 5
EZ, EX = NZ + 2 * HZ, BX + 16
X0 = 8
CZ, CX, CY = 8, 16, 64
KZ, KX = CZ + 16, CX + 16
AROUND = [(z, x, y) for z in (-1, 0, 1) for x in (-1, 0, 1) for y in (-1, 0, 1) if z or x or y]
EDGES = [(-1, -1), (-1, 1), (1, -1), (1, 1)]
X_ROWS = [(0, i) for i in range(5)] + [(1, i) for i in range(4)]
EDGE_ROWS = [(f, j, i) for f in (0, 1) for j in range(1, 5) for i in range(1, 6 - f - j)]


def chebyshev_table(low_bound, sweeps):
    middle = 0.5 * (2.0 + low_bound)
    radius = 0.5 * (2.0 - low_bound)
    quotient = middle / radius
    previous = 1.0 / quotient
    coeffs = []
    for number in range(sweeps):
        current = 1.0 / (2.0 * quotient - previous)
        coeffs.append((current * previous, 2.0 * current / radius))
        previous = current
    return (1.0 / middle, coeffs)


def lanes_of(rows):
    return lax.broadcasted_iota(jnp.int32, (rows, 128), 1)


def face(total):
    return 2.0 / jnp.maximum(total, 1e-3)


def kernel(
    right_ref, phase_ref, scale_ref, out_ref, coarse_ref, phase, scale,
    e0, e1, s0, s1, r0, r1, fz0, fz1, fx0, fx1, fy0, fy1, gy0, gy1, ig0, ig1,
    xsend, xrecv, esend, erecv, pack, unpack, stage,
    cp, cpack, cps, crp, rpack, crs, cs, cr, ci, sx, rx, cx,
    fetch_sem, send_sem, recv_sem,
):
    b = lax.axis_index("xy")
    g = lax.axis_index("gz")
    row, col = b // PY, b % PY
    n_rows = lax.axis_size("xy") // PY
    n_gz = lax.axis_size("gz")
    there = ((g > 0, g < n_gz - 1), (row > 0, row < n_rows - 1), (col > 0, col < PY - 1))

    def exists(d):
        found = None
        for axis in (0, 1, 2):
            if d[axis]:
                flag = there[axis][1 if d[axis] > 0 else 0]
                found = flag if found is None else found & flag
        return found

    def device(d):
        return {"xy": b + PY * d[1] + d[2], "gz": g + d[0]}

    sent = []

    def message(number, d, source, target):
        copy = pltpu.make_async_remote_copy(
            src_ref=source, dst_ref=target,
            send_sem=send_sem.at[number], recv_sem=recv_sem.at[number],
            device_id=device(d), device_id_type=pl.DeviceIdType.MESH,
        )
        back = tuple(-v for v in d)
        sent.append((d, copy))
        pl.when(exists(d))(copy.start)
        return lambda: pl.when(exists(back))(copy.wait_recv)

    barrier = pltpu.get_barrier_semaphore()
    count = jnp.int32(0)
    for d in AROUND:
        count = count + exists(d).astype(jnp.int32)

        @pl.when(exists(d))
        def _():
            pl.semaphore_signal(barrier, inc=1, device_id=device(d), device_id_type=pl.DeviceIdType.MESH)

    fetched = [
        pltpu.make_async_copy(source, target, fetch_sem.at[n])
        for n, (source, target) in enumerate((
            (phase_ref.at[:, 0], phase), (scale_ref.at[:, 0], scale),
            (right_ref.at[:, 0], e0.at[1, pl.ds(HZ, NZ), pl.ds(X0, BX)]),
        ))
    ]
    for copy in fetched:
        copy.start()

    def clear(ref, *at):
        ref[at] = jnp.zeros(ref.at[at].shape, jnp.float32)

    def clear_without(d, ref, *at):
        @pl.when(jnp.logical_not(exists(d)))
        def _():
            clear(ref, *at)

    for f in (0, 1):
        for p in range(EZ):
            clear(e0, f, p, slice(0, X0))
            clear(e0, f, p, slice(X0 + BX, EX))
            if p < HZ or p >= HZ + NZ:
                clear_without((-1 if p < HZ else 1, 0, 0), e0, f, p, slice(X0, X0 + BX))
    for d in AROUND:
        dz, dx, dy = d
        if dy:
            groups = {-1: (0,), 0: (1, 2), 1: (3,)}[dz]
            rows = {-1: slice(0, X0), 0: slice(X0, X0 + BX), 1: slice(X0 + BX, EX)}[dx]
            for a in groups:
                clear_without(d, unpack, 0 if dy > 0 else 1, a, rows)

    for copy in fetched:
        copy.wait()
    for z in range(NZ):
        heavy = jnp.where(phase[z] == 1, 1000.0, 1.0).astype(jnp.float32)
        e0[0, HZ + z, X0:X0 + BX] = heavy * scale[z]

    for j, (f, away) in enumerate(X_ROWS):
        xsend[0, j] = e0[f, HZ:HZ + NZ, X0 + away, :]
        xsend[1, j] = e0[f, HZ:HZ + NZ, X0 + BX - 1 - away, :]

    for q, (dz, dx) in enumerate(EDGES):
        for n, (f, j, i) in enumerate(EDGE_ROWS):
            p = HZ + NZ - j if dz > 0 else HZ + j - 1
            r = X0 + BX - i if dx > 0 else X0 + i - 1
            esend[q, n:n + 1] = e0[f, p, r:r + 1, :]

    lane = lanes_of(BX)

    for a in (0, 1):
        packed = [None, None]
        for i in range(8):
            for f in (0, 1):
                v = e0[f, HZ + 8 * a + i, X0:X0 + BX]
                at = 16 * i + 8 * f
                for side in (0, 1):
                    rolled = pltpu.roll(v, (at + 8 * side) % 128, 1)
                    packed[side] = rolled if packed[side] is None else jnp.where(lane < at, packed[side], rolled)
        pack[0, a], pack[1, a] = packed

    for p in range(KZ):
        for f in (0, 1):
            clear(cp, f, p)
        for side in (0, 1):
            if p < 6:
                clear(cps, side, p)
            if p < 3:
                clear(crs, side, p)
        if p < 12:
            clear(crp, p)

    pl.semaphore_wait(barrier, count)

    first_waits, waits = [], []
    order = sorted(range(26), key=lambda n: (-abs(AROUND[n][1]), abs(AROUND[n][0]) + abs(AROUND[n][2])))
    for n in order:
        d = dz, dx, dy = AROUND[n]
        if abs(dz) + abs(dx) + abs(dy) > 1:
            continue
        if dx:
            side = (dx + 1) // 2
            source, target = xsend.at[side, pl.ds(0, 1)], xrecv.at[side, pl.ds(0, 1)]
        elif dz:
            source = e0.at[0, HZ + NZ - 1 if dz > 0 else HZ, pl.ds(X0, BX)]
            target = e0.at[0, HZ - 1 if dz > 0 else HZ + NZ, pl.ds(X0, BX)]
        else:
            side = (dy + 1) // 2
            source, target = pack.at[side], unpack.at[side, pl.ds(1, 2), pl.ds(X0, BX)]
        first_waits.append(message(n, d, source, target))
    for n in order:
        d = dz, dx, dy = AROUND[n]
        if dy and (dz or dx):
            side = (dy + 1) // 2
            size = 1 if dz else 2
            from_group, to_group = {1: (1, 0), -1: (0, 3), 0: (0, 1)}[dz]
            from_row, rows = {1: (BX - 8, 8), -1: (0, 8), 0: (0, BX)}[dx]
            to_row = {1: 0, -1: X0 + BX, 0: X0}[dx]
            source = pack.at[side, pl.ds(from_group, size), pl.ds(from_row, rows)]
            target = unpack.at[side, pl.ds(to_group, size), pl.ds(to_row, rows)]
            waits.append(message(n, d, source, target))
        elif dz and dx:
            q = EDGES.index((dz, dx))
            waits.append(message(n, d, esend.at[q], erecv.at[q]))
        elif dx:
            side = (dx + 1) // 2
            waits.append(message(78 + side, d, xsend.at[side, pl.ds(1, 8)], xrecv.at[side, pl.ds(1, 8)]))
        elif dz:
            side = (dz + 1) // 2
            for f in (0, 1):
                if dz > 0:
                    source, target = HZ + NZ - 5 + f, f
                else:
                    source, target = HZ + 1 - f, HZ + NZ + 1 - f
                waits.append(message(
                    80 + 2 * f + side, d,
                    e0.at[f, pl.ds(source, 4), pl.ds(X0, BX)],
                    e0.at[f, pl.ds(target, 4), pl.ds(X0, BX)],
                ))

    def place_rows(numbers):
        for side in (0, 1):
            @pl.when(there[1][1 - side])
            def _():
                for j in numbers:
                    f, away = X_ROWS[j]
                    to = X0 + BX + away if side == 0 else X0 - 1 - away
                    e0[f, HZ:HZ + NZ, to, :] = xrecv[side, j]

    def unpack_plane(p, rows):
        a = (p + 3) // 8
        right, left = unpack[0, a, rows], unpack[1, a, rows]
        lane = lanes_of(right.shape[0])
        for f in (0, 1):
            at = 16 * ((p + 3) % 8) + 8 * f
            low = pltpu.roll(right, (128 - at) % 128, 1)
            high = pltpu.roll(left, (120 - at) % 128, 1)
            e1[f, p, rows] = jnp.where(lane < 8, low, jnp.where(lane >= 120, high, 0.0))

    for wait in first_waits:
        wait()
    place_rows([0])
    for p in range(HZ, HZ + NZ):
        unpack_plane(p, slice(X0, X0 + BX))

    lane8 = lanes_of(8)

    def y_low(v):
        a0, a1 = pltpu.roll(v[0], 1, 1), pltpu.roll(v[1], 1, 1)
        return jnp.where(lane8 == 0, a1, a0), jnp.where(lane8 == 0, a0, a1)

    def y_high(v):
        a0, a1 = pltpu.roll(v[0], 127, 1), pltpu.roll(v[1], 127, 1)
        return jnp.where(lane8 == 127, a1, a0), jnp.where(lane8 == 127, a0, a1)

    center, coeffs = chebyshev_table(0.5, FINE_SWEEPS)
    es, fzs, fxs, fys, gys, igs = (e0, e1), (fz0, fz1), (fx0, fx1), (fy0, fy1), (gy0, gy1), (ig0, ig1)

    def at_rows(refs, p, r, *lead):
        return [ref[(*lead, p, pl.ds(r, 8))] for ref in refs]

    tiles = [4 + 8 * i for i in range(5)]

    def plane_faces(p, below, rows_of, lanes):
        out = []
        for i, r in enumerate(rows_of):
            d = at_rows(es, p, r, 0)
            left, right = y_low(d), y_high(d)
            for k, t in enumerate(lanes):
                up = face(d[t] + es[t][0, p + 1, pl.ds(r, 8)])
                w, e = face(d[t] + es[t][0, p, pl.ds(r - 1, 8)]), face(d[t] + es[t][0, p, pl.ds(r + 1, 8)])
                v, h = face(d[t] + left[t]), face(d[t] + right[t])
                inverse = jnp.where(d[t] > 0.0, 1.0 / (below[len(lanes) * i + k] + up + w + e + v + h), 0.0)
                fzs[t][p + 1, pl.ds(r, 8)] = up
                fxs[t][p, pl.ds(r, 8)] = w
                if r == rows_of[-1]:
                    fxs[t][p, pl.ds(r + 1, 8)] = e
                fys[t][p, pl.ds(r, 8)] = v
                gys[t][p, pl.ds(r, 8)] = h
                igs[t][p, pl.ds(r, 8)] = inverse
                ss[t][0, p, pl.ds(r, 8)] = es[t][1, p, pl.ds(r, 8)] * inverse * center
                out.append(up)
        return tuple(out)

    def faces(first, end, rows_of, lanes):
        below = []
        for r in rows_of:
            for t in lanes:
                up = face(es[t][0, first - 1, pl.ds(r, 8)] + es[t][0, first, pl.ds(r, 8)])
                fzs[t][first, pl.ds(r, 8)] = up
                below.append(up)
        step = 4

        def some(j, below):
            for u in range(step):
                below = plane_faces(first + step * j + u, below, rows_of, lanes)
            return below

        lax.fori_loop(0, (end - first) // step, some, tuple(below))

    ss, rs = (s0, s1), (r0, r1)
    own_rows = [X0 + 8 * i for i in range(4)]
    faces(HZ, HZ + NZ, own_rows, (0,))

    dot_kw = dict(preferred_element_type=jnp.float32, precision=lax.Precision.HIGHEST)
    from_lane = lax.broadcasted_iota(jnp.int32, (128, 128), 0)
    to_lane = lax.broadcasted_iota(jnp.int32, (128, 128), 1)
    def ones(mask):
        return jnp.where(mask, 1.0, 0.0).astype(jnp.float32)

    pairs = (ones(from_lane // 2 == to_lane), ones(from_lane // 2 == to_lane - CY))
    evens = (ones(from_lane == 2 * to_lane), ones(from_lane == 2 * to_lane - 2 * CY))
    odds = ones(from_lane == 2 * to_lane + 1)

    def row_pairs(ref, p):
        return ref[p, pl.ds(X0, CX, stride=2), :] + ref[p, pl.ds(X0 + 1, CX, stride=2), :]

    for c in range(CZ):
        p = HZ + 2 * c
        rows = pl.ds(c * CX, CX)
        low_z, high_z = row_pairs(fz0, p), row_pairs(fz0, p + 2)
        low_x = fx0[p, pl.ds(X0, CX, stride=2), :] + fx0[p + 1, pl.ds(X0, CX, stride=2), :]
        high_x = fx0[p, pl.ds(X0 + 2, CX, stride=2), :] + fx0[p + 1, pl.ds(X0 + 2, CX, stride=2), :]
        stage[0, rows] = low_z
        stage[1, rows] = low_x
        stage[2, rows] = low_z + high_z + low_x + high_x
        stage[3, rows] = row_pairs(fy0, p) + row_pairs(fy0, p + 1)
        stage[4, rows] = row_pairs(gy0, p) + row_pairs(gy0, p + 1)

    first_pair = jnp.dot(stage[2], pairs[0], **dot_kw) + jnp.dot(stage[3], evens[0], **dot_kw)
    first_pair = first_pair + jnp.dot(stage[4], odds, **dot_kw)
    first_pair = first_pair + jnp.dot(stage[0], pairs[1], **dot_kw)
    second_pair = jnp.dot(stage[1], pairs[0], **dot_kw) + jnp.dot(stage[3], evens[1], **dot_kw)
    fields = [(v * 0.0625).reshape(CZ, CX, 128) for v in (first_pair, second_pair)]
    cp[0, 8:8 + CZ, 8:8 + CX], cp[1, 8:8 + CZ, 8:8 + CX] = fields
    clane = lanes_of(CX)
    for a in (0, 1):
        packed = [None, None]
        for i in range(4):
            for f in range(4):
                at = 32 * i + 8 * f
                for side in (0, 1):
                    shift = (at - 64 * (f % 2) - 56 * side) % 128
                    rolled = pltpu.roll(fields[f // 2][4 * a + i], shift, 1)
                    packed[side] = rolled if packed[side] is None else jnp.where(clane < at, packed[side], rolled)
        cpack[0, a], cpack[1, a] = packed

    def coarse_messages(number, depth, array, strips_from, strips_to):
        lead = (slice(None),) if len(array.shape) == 4 else ()
        groups = strips_from.shape[1]
        waits = []
        for n in order:
            d = dz, dx, dy = AROUND[n]
            from_row, to_row, rows = {1: (8, 0, 8), -1: (0, 24, 8), 0: (0, 8, CX)}[dx]
            block = {1: 0, -1: 2, 0: 1}[dz]
            if dy:
                side = (dy + 1) // 2
                source = strips_from.at[side, :, pl.ds(from_row, rows)]
                target = strips_to.at[side, pl.ds(groups * block, groups), pl.ds(to_row, rows)]
            else:
                source = array.at[(*lead, pl.ds(depth, depth), pl.ds(8 + from_row, rows))]
                target = array.at[(*lead, pl.ds(depth * block, depth), pl.ds(to_row, rows))]
            waits.append(message(number + n, d, source, target))
        return waits

    def along(number, axis, source_of, target_of):
        waits = []
        for side in (0, 1):
            d = tuple((2 * side - 1) if k == axis else 0 for k in range(3))
            waits.append(message(number + side, d, source_of(side), target_of(side)))
        return waits

    edge, halo = (8, 16), (24, 0)
    planes_own, groups_own = pl.ds(8, CZ), pl.ds(2, 2)
    y_waits = along(
        26, 2, lambda side: cpack.at[side], lambda side: cps.at[side, groups_own, pl.ds(8, CX)]
    )
    x_waits = along(
        28, 1, lambda side: cp.at[:, planes_own, pl.ds(edge[side], 8)],
        lambda side: cp.at[:, planes_own, pl.ds(halo[side], 8)],
    )
    face_waits = along(
        30, 0, lambda side: cp.at[:, planes_own, pl.ds(8, CX)],
        lambda side: cp.at[:, pl.ds((16, 0)[side], CZ), pl.ds(8, CX)],
    )
    for wait in y_waits:
        wait()
    x_waits += along(
        32, 1, lambda side: cps.at[:, groups_own, pl.ds(edge[side], 8)],
        lambda side: cps.at[:, groups_own, pl.ds(halo[side], 8)],
    )


    for wait in waits:
        wait()
    place_rows(range(1, 9))
    for q, (dz, dx) in enumerate(EDGES):
        @pl.when(exists((-dz, -dx, 0)))
        def _():
            for n, (f, j, i) in enumerate(EDGE_ROWS):
                p = HZ - j if dz > 0 else HZ + NZ + j - 1
                r = X0 - i if dx > 0 else X0 + BX + i - 1
                e0[f, p, r:r + 1, :] = erecv[q, n:n + 1]

    for p in range(EZ):
        if HZ <= p < HZ + NZ:
            unpack_plane(p, slice(0, X0))
            unpack_plane(p, slice(X0 + BX, EX))
        else:
            unpack_plane(p, slice(0, EX))
    faces(HZ, HZ + NZ, [4], (0,))
    faces(HZ, HZ + NZ, [36], (0,))
    faces(HZ, HZ + NZ, tiles, (1,))
    faces(1, HZ, tiles, (0, 1))
    faces(HZ + NZ, EZ - 1, tiles, (0, 1))

    def sweep(k):
        first, end = 2 + k, EZ - 2 - k
        unroll = next(n for n in (5, 4, 3, 2) if (end - first) % n == 0)
        keep, push = coeffs[k]
        rows_of = tiles if k + 1 < FINE_SWEEPS else [X0 + 8 * i for i in range(4)]
        lanes = (0, 1) if k + 1 < FINE_SWEEPS else (0,)
        source = (lambda t, p, r: es[t][1, p, pl.ds(r, 8)]) if k == 0 else (lambda t, p, r: rs[t][k - 1, p, pl.ds(r, 8)])

        def step(j, fluxes):
            fluxes = list(fluxes)
            for i, r in enumerate(rows_of):
                for u in range(unroll):
                    p = first + unroll * j + u
                    c = at_rows(ss, p, r, k)
                    left, right = y_low(c), y_high(c)
                    for t in lanes:
                        up = fzs[t][p + 1, pl.ds(r, 8)] * (ss[t][k, p + 1, pl.ds(r, 8)] - c[t])
                        total = fluxes[len(lanes) * i + t] - up
                        total = total + fxs[t][p, pl.ds(r, 8)] * (c[t] - ss[t][k, p, pl.ds(r - 1, 8)])
                        total = total + fxs[t][p, pl.ds(r + 1, 8)] * (c[t] - ss[t][k, p, pl.ds(r + 1, 8)])
                        total = total + fys[t][p, pl.ds(r, 8)] * (c[t] - left[t])
                        total = total + gys[t][p, pl.ds(r, 8)] * (c[t] - right[t])
                        residual = source(t, p, r) - total
                        rs[t][k, p, pl.ds(r, 8)] = residual
                        if k + 1 < FINE_SWEEPS:
                            ss[t][k + 1, p, pl.ds(r, 8)] = keep * c[t] + (push * residual) * igs[t][p, pl.ds(r, 8)]
                        fluxes[len(lanes) * i + t] = up
            return tuple(fluxes)

        fluxes = []
        for r in rows_of:
            for t in lanes:
                fluxes.append(
                    fzs[t][first, pl.ds(r, 8)] * (ss[t][k, first, pl.ds(r, 8)] - ss[t][k, first - 1, pl.ds(r, 8)])
                )
        lax.fori_loop(0, (end - first) // unroll, step, tuple(fluxes))

    sweep(0)
    sweep(1)
    sweep(2)
    for wait in x_waits:
        wait()
    for n, r in ((34, 0), (36, 24)):
        face_waits += along(
            n, 0, lambda side: cp.at[:, planes_own, pl.ds(r, 8)],
            lambda side: cp.at[:, pl.ds((16, 0)[side], CZ), pl.ds(r, 8)],
        )
    face_waits += along(
        38, 0, lambda side: cps.at[:, groups_own], lambda side: cps.at[:, pl.ds((4, 0)[side], 2)]
    )
    sweep(3)

    last_residual = rs[0].at[FINE_SWEEPS - 1]
    for c in range(CZ):
        p = HZ + 2 * c
        stage[0, pl.ds(c * CX, CX)] = row_pairs(last_residual, p) + row_pairs(last_residual, p + 1)
    half = CZ * CX // 2
    planes = jnp.dot(stage[0, 0:half], pairs[0], **dot_kw) + jnp.dot(stage[0, half:2 * half], pairs[1], **dot_kw)
    planes = (planes * 0.125).reshape(CZ // 2, CX, 128)
    crp[4:8, 8:8 + CX] = planes
    packed = [None, None]
    for z in range(CZ):
        for side in (0, 1):
            rolled = pltpu.roll(planes[z % 4], (8 * z - 64 * (z // 4) - 56 * side) % 128, 1)
            packed[side] = rolled if packed[side] is None else jnp.where(clane < 8 * z, packed[side], rolled)
    rpack[0, 0], rpack[1, 0] = packed
    right_waits = coarse_messages(52, CZ // 2, crp, rpack, crs)

    xlane = lanes_of(KX)

    def widen(base, second, right, left, at):
        base = pltpu.roll(base, 64, 1) if second else base
        right = pltpu.roll(right, (64 - at) % 128, 1)
        left = pltpu.roll(left, (120 - at) % 128, 1)
        return jnp.where(xlane < CY, base, jnp.where(xlane < 96, right, left))

    for wait in face_waits:
        wait()
    for p in range(KZ):
        for f in range(4):
            cs[f, p, 0:KX] = widen(
                cp[f // 2, p], f % 2, cps[0, p // 4], cps[1, p // 4], 32 * (p % 4) + 8 * f
            )
        diagonal = cs[0, p, 0:KX]
        ci[p, 0:KX] = jnp.where(diagonal > 0.0, 1.0 / diagonal, 0.0)

    for wait in right_waits:
        wait()
    center, ccoeffs = chebyshev_table(0.1, COARSE_SWEEPS)
    for p in range(KZ):
        z = p % 8
        value = widen(crp[4 * (p // 8) + z % 4], z // 4, crs[0, p // 8], crs[1, p // 8], 8 * z)
        cr[p, 0:KX] = value
        sx[0, p, 0:KX] = value * ci[p, 0:KX] * center

    def coarse_sweep(k):
        halo = COARSE_SWEEPS - 2 - k
        first, count = 8 - halo, CZ + 2 * halo
        n_tiles = (CX + 2 * halo + 7) // 8
        r_first = min(8 - halo, KX + 7 - 8 * n_tiles)
        rows_of = [r_first + 8 * i for i in range(n_tiles)]
        keep, push = ccoeffs[k]
        unroll = count // 2

        def step(j, fluxes):
            fluxes = list(fluxes)
            for i, r in enumerate(rows_of):
                rows = pl.ds(r, 8)
                for u in range(unroll):
                    p = first + unroll * j + u
                    c = sx[k, p, rows]
                    above = sx[k, p + 1, rows]
                    fz = cs[1, p + 1, rows]
                    fy = cs[3, p, rows]
                    total = cs[0, p, rows] * c - fluxes[i] - fz * above
                    total = total - cs[2, p, rows] * sx[k, p, pl.ds(r - 1, 8)]
                    total = total - cs[2, p, pl.ds(r + 1, 8)] * sx[k, p, pl.ds(r + 1, 8)]
                    total = total - fy * pltpu.roll(c, 1, 1) - pltpu.roll(fy * c, 127, 1)
                    residual = (cr if k == 0 else rx.at[k])[p, rows] - total
                    if k + 2 < COARSE_SWEEPS:
                        rx[k + 1, p, rows] = residual
                    sx[k + 1, p, rows] = keep * c + (push * residual) * ci[p, rows]
                    fluxes[i] = fz * c
            return tuple(fluxes)

        lax.fori_loop(
            0, count // unroll, step,
            tuple(cs[1, first, pl.ds(r, 8)] * sx[k, first - 1, pl.ds(r, 8)] for r in rows_of),
        )

    for k in range(COARSE_SWEEPS - 1):
        coarse_sweep(k)
    for z in range(CZ):
        mine = sx[0, 8 + z, 8:8 + CX]
        for k in range(1, COARSE_SWEEPS):
            mine = mine + sx[k, 8 + z, 8:8 + CX]
        cx[z] = jnp.where(clane < CY, mine, 0.0)

    spread = jnp.where(to_lane // 2 == from_lane, 1.0, 0.0).astype(jnp.float32)
    stage[1] = jnp.dot(cx[...].reshape(CZ * CX, 128), spread, **dot_kw)

    for c in range(CZ):
        coarse_ref[c, 0] = cx[c, :, 0:CY]
        wide_rows = stage[1, pl.ds(c * CX, CX), :]
        spot = pl.ds(BX * (c % 2), CX, stride=2), pl.ds(BX * (c % 2) + 1, CX, stride=2)
        stage[2, spot[0], :] = wide_rows
        stage[2, spot[1], :] = wide_rows
        twice = stage[2, pl.ds(BX * (c % 2), BX), :]
        for i in (0, 1):
            mine = s0[0, HZ + 2 * c + i, X0:X0 + BX]
            for k in range(1, FINE_SWEEPS):
                mine = mine + s0[k, HZ + 2 * c + i, X0:X0 + BX]
            out_ref[2 * c + i, 0] = mine + twice

    for d, copy in sent:
        pl.when(exists(d))(copy.wait_send)


def body(right_side, phase, density_scale):
    fine = pltpu.VMEM((EZ, EX, 128), jnp.float32)
    return pl.pallas_call(
        kernel,
        out_shape=(
            jax.ShapeDtypeStruct((NZ, 1, BX, BY), jnp.float32),
            jax.ShapeDtypeStruct((CZ, 1, CX, CY), jnp.float32),
        ),
        in_specs=[pl.BlockSpec(memory_space=pltpu.HBM)] * 3,
        out_specs=(pl.BlockSpec(memory_space=pltpu.VMEM),) * 2,
        scratch_shapes=[
            pltpu.VMEM((NZ, BX, BY), jnp.int32),
            pltpu.VMEM((NZ, BX, BY), jnp.float32),
            pltpu.VMEM((2, EZ, EX, 128), jnp.float32),
            pltpu.VMEM((2, EZ, EX, 128), jnp.float32),
            *([pltpu.VMEM((FINE_SWEEPS, EZ, EX, 128), jnp.float32)] * 4),
            *([fine] * 10),
            pltpu.VMEM((2, 9, NZ, 128), jnp.float32),
            pltpu.VMEM((2, 9, NZ, 128), jnp.float32),
            pltpu.VMEM((4, 16, 128), jnp.float32),
            pltpu.VMEM((4, 16, 128), jnp.float32),
            pltpu.VMEM((2, 2, BX, 128), jnp.float32),
            pltpu.VMEM((2, 4, EX, 128), jnp.float32),
            pltpu.VMEM((5, CZ * CX, 128), jnp.float32),
            pltpu.VMEM((2, KZ, KX, 128), jnp.float32),
            pltpu.VMEM((2, 2, CX, 128), jnp.float32),
            pltpu.VMEM((2, 6, KX, 128), jnp.float32),
            pltpu.VMEM((12, KX, 128), jnp.float32),
            pltpu.VMEM((2, 1, CX, 128), jnp.float32),
            pltpu.VMEM((2, 3, KX, 128), jnp.float32),
            pltpu.VMEM((4, KZ, KX + 8, 128), jnp.float32),
            pltpu.VMEM((KZ, KX + 8, 128), jnp.float32),
            pltpu.VMEM((KZ, KX + 8, 128), jnp.float32),
            pltpu.VMEM((COARSE_SWEEPS, KZ, KX + 8, 128), jnp.float32),
            pltpu.VMEM((COARSE_SWEEPS, KZ, KX + 8, 128), jnp.float32),
            pltpu.VMEM((CZ, CX, 128), jnp.float32),
            pltpu.SemaphoreType.DMA((3,)),
            pltpu.SemaphoreType.DMA((84,)),
            pltpu.SemaphoreType.DMA((84,)),
        ],
        compiler_params=pltpu.CompilerParams(
            collective_id=0, has_side_effects=True, vmem_limit_bytes=107 << 19
        ),
        name="vcycle",
    )(right_side, phase, density_scale)


def solution(mesh):
    placed = P("gz", "xy", None, None)
    return jax.shard_map(
        body,
        mesh=mesh,
        in_specs=(placed, placed, placed),
        out_specs=(placed, placed),
        check_vma=False,
    )
```
